128 devices in a mesh: grp: 4 (over z), dev: 32 (over x, y, core).
Axes of the slice: x: 4, y: 4, z: 4, core: 2. Of those that a mesh axis runs over, the one named last changes fastest.
Arguments:
- fitted_factors: bfloat16 [9000, 32768], P(None, 'dev'), may hold values from -0.0625 to 0.0625
- panel_blocks: int32 [16], P('grp'), may hold values from 0 to 127
- kept_tiles: int32 [16, 256], P('grp', 'dev'), may hold values 0 or 1
- tile_owner: int32 [4, 32, 32, 1], P('grp', 'dev'), may hold values from 0 to 31; in each aligned block of 32 rows (0 to 31, 32 to 63, ..., all dimensions but the last counted through in order) at most 2 rows name the same one
Outputs:
- exported: bfloat16 [4, 32, 64, 256, 128], P('grp', 'dev')
The draws below stay inside these ranges and needn't reach their ends.
Inputs may be any that keep to these rules, and one draw needn't show every extreme that they name: `tile_owner`: in each device's list of 32 tiles no owner appears more than 2 times, and some owner appears exactly 2 times.
All inputs are finite; a program needn't handle non-finite values. No bound on the sum of `kept_tiles` on one device may be relied on, other than what follows from the above.
Results may differ from the reference program's by a relative error of at most 0.0015.
Values may be sent and summed in bfloat16 or wider, within the bound.
No kernel may reach another device: no remote copies, remote signals or barrier semaphores. Data moves between devices by JAX's collectives and lax.ppermute only.
A program may use at most 128 MiB of HBM per device.

```python
import math
import jax
import jax.numpy as jnp
import numpy as np
from jax import lax

NAUX = 9000
PB = 256
CB = 128
BLK_DEV = 8
PANEL_GRP = 4
TILES_DEV = 32
CAP = 2
NCB = 256
NPAIR = 32768
NPANEL = 128
PANELS = 16
N_GRP = 4
N_DEV = 32


def touch_ends(drawn, rng, smallest, top_value):
    index_at = [jax.random.randint(jax.random.fold_in(rng, axis), (), 0, length) for axis, length in enumerate(drawn.shape)]
    longest = drawn.shape.index(max(drawn.shape))
    neighbour = index_at[:longest] + [(index_at[longest] + 1) % drawn.shape[longest]] + index_at[longest + 1:]
    return drawn.at[tuple(index_at)].set(smallest).at[tuple(neighbour)].set(top_value)


def shard_levels(key, shape, cuts, smallest, top_value):
    gain, own = 1.0, jax.random.fold_in(key, 6)
    for axis_at, parts in cuts:
        steps = jnp.exp(jax.random.uniform(jax.random.fold_in(own, axis_at), (parts,), jnp.float32, smallest / len(cuts), top_value / len(cuts)))
        gain = gain * jnp.repeat(steps, shape[axis_at] // parts).reshape([-1 if axis == axis_at else 1 for axis in range(len(shape))])
    return gain


def routed_block(key, own, number, rows, number_of, top, reach, skew):
    ranking = jax.random.permutation(key, number_of)
    packed, usual = load_shares(number_of, rows * top, reach, skew, True), load_shares(number_of, rows * top, reach, skew, False)
    places = jnp.arange(number_of)

    def named(sizes, offset_by):
        used = int((sizes > 0).sum())
        fixed = max(1, used // 4)
        passed = fixed + (places - fixed + offset_by * (used - fixed)) % max(1, number_of - fixed)
        return jnp.zeros((number_of,), jnp.int32).at[ranking[jnp.where(places < fixed, places, passed)]].set(jnp.asarray(sizes, jnp.int32))

    sizes = jnp.where(number % 4 == 0, named(packed, number // 4), named(usual, number - number // 4 - 1))
    mixed = jax.random.permutation(jax.random.fold_in(own, 3), number_of)
    giver, sink = mixed[0:number_of // 2 * 2:2], mixed[1:number_of // 2 * 2:2]
    slack = jnp.minimum(sizes[giver] - 1, reach - sizes[sink]) // 2
    slack = jnp.where((giver == ranking[0]) | (sink == ranking[0]) | (sizes[sink] == 0), 0, jnp.maximum(slack, 0))
    passed = jax.random.randint(jax.random.fold_in(own, 4), (number_of // 2,), 0, 1 << 20) % (slack + 1)
    sizes = sizes.at[giver].add(-passed).at[sink].add(passed)
    labels = jnp.searchsorted(jnp.cumsum(sizes), jnp.arange(rows * top), side="right").astype(jnp.int32)
    table = labels.reshape(top, rows).T
    table = table[jax.random.permutation(jax.random.fold_in(own, 1), rows)]
    offset_by = jax.random.randint(jax.random.fold_in(own, 2), (rows, 1), 0, top)
    return jnp.take_along_axis(table, (jnp.arange(top)[None, :] + offset_by) % top, axis=1)


def load_shares(number_of, total, most, skew, full):
    portions = [(1 << 20) // math.isqrt(standing ** skew) + 1 for standing in range(1, number_of + 1)]
    largest = most if full else min(most, max(-(-total // number_of), total * portions[0] // sum(portions)))
    least = 1 if total - largest >= number_of - 1 else 0
    counts, rest = [largest] + [least] * (number_of - 1), total - largest - least * (number_of - 1)
    while rest > 0:
        movable = [i for i in range(1, number_of) if counts[i] < largest] or [i for i in range(1, number_of) if counts[i] < most]
        pool, left = sum([portions[i] for i in movable]), rest
        for i in movable:
            extra = min(most - counts[i], max(1, left * portions[i] // pool), rest)
            counts[i] = counts[i] + extra
            rest = rest - extra
    return np.array(counts)


def centred(own_key, extent, deviation, reach, cuts=(), kind=jnp.bfloat16):
    level = shard_levels(own_key, extent, cuts, -0.22, 0.18) if cuts else 1.0
    result = jax.random.normal(own_key, extent, jnp.float32) * deviation * level
    return jnp.minimum(jnp.maximum(result, -reach), reach).astype(kind)


def setup_inputs(seed: int = 0) -> dict:
    keys = jax.random.split(jax.random.key(seed), 5)
    fitted_factors = centred(keys[0], (NAUX, NPAIR), NAUX ** -0.5, 0.0625, ((1, 32),))
    panel_blocks = touch_ends(jax.random.randint(keys[1], (PANELS,), 0, NPANEL), jax.random.fold_in(keys[1], 1), 0, NPANEL - 1).astype(jnp.int32)
    kept_tiles = touch_ends((jax.random.randint(keys[2], (PANELS, NCB), 0, 5) < 4).astype(jnp.int32), jax.random.fold_in(keys[2], 1), 0, 1)
    tile_owner_keys = jax.random.split(jax.random.fold_in(keys[3], 1), N_GRP * N_DEV * TILES_DEV // TILES_DEV)
    tile_owner_turns = jax.random.permutation(jax.random.fold_in(keys[3], 3), N_GRP * N_DEV * TILES_DEV // TILES_DEV)
    tile_owner = jax.vmap(lambda own, number: routed_block(jax.random.fold_in(keys[3], 2), own, number, TILES_DEV, N_DEV, 1, CAP, 2))(tile_owner_keys, tile_owner_turns).reshape((N_GRP, N_DEV, TILES_DEV, 1))
    return dict(fitted_factors=fitted_factors, panel_blocks=panel_blocks, kept_tiles=kept_tiles, tile_owner=tile_owner)


def slot_ranks(owners):
    count = owners.shape[-1]
    same_owner = owners[..., :, None] == owners[..., None, :]
    earlier = jnp.arange(count)[None, :] < jnp.arange(count)[:, None]
    return jnp.sum((same_owner & earlier).astype(jnp.int32), axis=-1).astype(jnp.int32)


def reference(fitted_factors, panel_blocks, kept_tiles, tile_owner):
    def panel_row(operands):
        block_idx, kept_row = operands
        panel_cols = lax.dynamic_slice_in_dim(fitted_factors, (block_idx * PB).astype(jnp.int32), PB, 1)
        product = lax.dot_general(panel_cols, fitted_factors, (((0,), (0,)), ((), ())), preferred_element_type=jnp.float32)
        product = product.reshape(PB, NCB, CB) * kept_row.astype(jnp.float32)[None, :, None]
        return jnp.transpose(product.astype(jnp.bfloat16), (1, 0, 2))

    tile_all = lax.map(panel_row, (panel_blocks, kept_tiles))
    tile_all = tile_all.reshape(N_GRP, PANEL_GRP, N_DEV, BLK_DEV, PB, CB)
    tile_all = jnp.transpose(tile_all, (0, 2, 1, 3, 4, 5)).reshape(N_GRP, N_DEV, TILES_DEV, PB, CB)
    owners = tile_owner[..., 0]
    ranks = slot_ranks(owners)
    group_idx = jnp.broadcast_to(jnp.arange(N_GRP, dtype=jnp.int32)[:, None, None], owners.shape)
    source_idx = jnp.broadcast_to(jnp.arange(N_DEV, dtype=jnp.int32)[None, :, None], owners.shape)
    exported = jnp.zeros((N_GRP, N_DEV, N_DEV * CAP, PB, CB), jnp.bfloat16)
    return exported.at[group_idx, owners, source_idx * CAP + ranks].set(tile_all)
```

```python
import functools

import jax
import jax.numpy as jnp
from jax import lax
from jax.experimental import pallas as pl
from jax.experimental.pallas import tpu as pltpu
from jax.sharding import PartitionSpec as P

PB = 256
CB = 128
W = 128
CHUNKS = PB // W
PANELS = 4
C = PANELS * W
NAUX = 9000
HALF = 4608
QUART = HALF // 4
SIXT = QUART // 4
X, Y = 4, 4


def dev_id(x, y, core):
    return ((x % X) * Y + (y % Y)) * 2 + core


def ring_pairs(first, shift):
    pairs = []
    for x in range(X):
        for y in range(Y):
            for core in range(2):
                along_x = first == (core == 0)
                dx, dy = (shift, 0) if along_x else (0, shift)
                pairs.append((dev_id(x, y, core), dev_id(x + dx, y + dy, core)))
    return pairs


CORE_PAIRS = [(d, d ^ 1) for d in range(2 * X * Y)]


def move(value, first, shift):
    return lax.ppermute(value, "dev", ring_pairs(first, shift))


def swap(value):
    return lax.ppermute(value, "dev", CORE_PAIRS)


def pick_kernel(where_ref, *refs):
    ins, (own_ref, send_ref) = refs[:-2], refs[-2:]
    for i in range(PANELS):
        own_ref[:, i * W : (i + 1) * W] = ins[i][...]
        send_ref[:, i * W : (i + 1) * W] = ins[PANELS + i][...]


def pick(factors, col_blocks, core):
    rows = QUART
    steps = HALF // rows
    where = jnp.concatenate([col_blocks, core[None]]).astype(jnp.int32)

    def own_map(i, r, s):
        return (s[PANELS] * steps + r, s[i])

    def other_map(i, r, s):
        return ((1 - s[PANELS]) * steps + r, s[i])

    in_specs = [pl.BlockSpec((rows, W), functools.partial(own_map, i)) for i in range(PANELS)]
    in_specs += [pl.BlockSpec((rows, W), functools.partial(other_map, i)) for i in range(PANELS)]
    out_spec = pl.BlockSpec((rows, C), lambda r, s: (r, 0))
    shape = jax.ShapeDtypeStruct((HALF, C), jnp.bfloat16)
    return pl.pallas_call(
        pick_kernel,
        grid_spec=pltpu.PrefetchScalarGridSpec(
            num_scalar_prefetch=1, grid=(steps,), in_specs=in_specs, out_specs=[out_spec, out_spec]
        ),
        out_shape=[shape, shape],
        compiler_params=pltpu.CompilerParams(vmem_limit_bytes=32 << 20),
        cost_estimate=pl.CostEstimate(flops=0, bytes_accessed=4 * HALF * C * 2, transcendentals=0),
        name="pick_columns",
    )(where, *([factors] * (2 * PANELS)))


def export_kernel(tile_ref, scale_ref, prod_ref, out_ref):
    def slot(s, carry):
        t = tile_ref[s]
        row = pl.multiple_of((t // 8) * W, W)
        col = pl.multiple_of((t % 8) * CB, CB)
        block = prod_ref[pl.ds(row, W), pl.ds(col, CB)]
        out_ref[s] = (block * scale_ref[s]).astype(jnp.bfloat16)
        return carry

    lax.fori_loop(0, out_ref.shape[0], slot, 0)


def to_slots(product, tile_of, scale_of):
    slots = tile_of.shape[0]
    return pl.pallas_call(
        export_kernel,
        in_specs=[
            pl.BlockSpec(memory_space=pltpu.SMEM),
            pl.BlockSpec(memory_space=pltpu.SMEM),
            pl.BlockSpec(memory_space=pltpu.VMEM),
        ],
        out_specs=pl.BlockSpec(memory_space=pltpu.VMEM),
        out_shape=jax.ShapeDtypeStruct((slots, W, CB), jnp.bfloat16),
        compiler_params=pltpu.CompilerParams(vmem_limit_bytes=32 << 20),
        cost_estimate=pl.CostEstimate(
            flops=slots * W * CB, bytes_accessed=product.size * 4 + slots * W * CB * 2, transcendentals=0
        ),
        name="tiles_to_slots",
    )(tile_of, scale_of, product)


def rows_at(value, start, count):
    return lax.dynamic_slice_in_dim(value, start, count, 0)


def scatter_ring(take, size, here, root, first):
    half = size // 2
    far = ((here + 2) % 4) * size
    ahead, behind = (here + 1) % 4, (here + 3) % 4
    from_behind = move(take(far, half), first, 1)
    from_ahead = move(take(far + half, half), first, -1)
    root_behind, root_ahead = root == behind, root == ahead
    forth = jnp.concatenate(
        [jnp.where(root_behind, from_behind, take(ahead * size, half)), take(ahead * size + half, half)], axis=0
    )
    back = jnp.concatenate(
        [take(behind * size, half), jnp.where(root_ahead, from_ahead, take(behind * size + half, half))], axis=0
    )
    got_behind = move(forth, first, 1)
    got_ahead = move(back, first, -1)
    own = take(here * size, size)
    root_here = root == here
    low = jnp.where(root_here, own[:half], jnp.where(root_ahead, got_ahead[:half], got_behind[:half]))
    high = jnp.where(root_here, own[half:], jnp.where(root_behind, got_behind[half:], got_ahead[half:]))
    return jnp.concatenate([low, high], axis=0)


def gather_ring(piece, here, first):
    half = piece.shape[0] // 2
    from_behind = move(piece, first, 1)
    from_ahead = move(piece, first, -1)
    low = move(from_behind[:half], first, 1)
    high = move(from_ahead[half:], first, -1)
    far = jnp.concatenate([low, high], axis=0)
    return [(piece, here), (from_behind, (here + 3) % 4), (from_ahead, (here + 1) % 4), (far, (here + 2) % 4)]


def lay_out(pieces, base, buffer):
    for piece, place in pieces:
        buffer = lax.dynamic_update_slice_in_dim(buffer, piece, base + place * piece.shape[0], 0)
    return buffer


def slot_table(owners, slots, kept):
    count = owners.shape[0]
    same_owner = owners[:, None] == owners[None, :]
    earlier = jnp.arange(count)[None, :] < jnp.arange(count)[:, None]
    ranks = jnp.sum((same_owner & earlier).astype(jnp.int32), axis=-1)
    hit = (owners * 2 + ranks)[None, :] == jnp.arange(slots)[:, None]
    tile_of = jnp.sum(jnp.where(hit, jnp.arange(count)[None, :], 0), axis=1).astype(jnp.int32)
    scale_of = jnp.sum(jnp.where(hit, kept[None, :], 0), axis=1).astype(jnp.float32)
    return tile_of, scale_of


def body(fitted_factors, panel_blocks, kept_tiles, tile_owner):
    me = lax.axis_index("dev")
    core = me % 2
    mx, my = me // (2 * Y), (me // 2) % Y
    here_a, here_b = jnp.where(core == 0, mx, my), jnp.where(core == 0, my, mx)
    root = panel_blocks // 4
    root_x, root_y, root_core = root // (2 * Y), (root // 2) % Y, root % 2

    def per_column(value):
        return jnp.repeat(value, W)[None, :]

    root_a = per_column(jnp.where(core == 0, root_x, root_y))
    root_b = per_column(jnp.where(core == 0, root_y, root_x))
    is_mine = per_column(root_core == core)
    col_blocks = (panel_blocks % 4) * CHUNKS

    slots = 2 * 2 * X * Y
    tile_of, scale_of = slot_table(tile_owner[0, 0, :, 0], slots, kept_tiles.reshape(-1))

    received = []
    for h in range(CHUNKS):
        own, send = pick(fitted_factors, col_blocks + h, core)
        sibling = swap(send)

        def take(start, count):
            return jnp.where(is_mine, rows_at(own, start, count), rows_at(sibling, start, count))

        quart = scatter_ring(take, QUART, here_a, root_a, True)
        sixteenth = scatter_ring(functools.partial(rows_at, quart), SIXT, here_b, root_b, False)
        pieces = gather_ring(sixteenth, here_b, False)
        quart = lay_out(pieces, 0, jnp.zeros((QUART, C), jnp.bfloat16))
        pieces = gather_ring(quart, here_a, True)
        far_a = here_b
        others = [
            (swap(piece), (far_a + off) % 4) for (piece, _), off in zip(pieces, (0, 3, 1, 2), strict=True)
        ]
        panel = lay_out(pieces, core * HALF, jnp.zeros((2 * HALF, C), jnp.bfloat16))
        panel = lay_out(others, (1 - core) * HALF, panel)
        product = lax.dot_general(
            panel[:NAUX], fitted_factors, (((0,), (0,)), ((), ())), preferred_element_type=jnp.float32
        )
        outgoing = to_slots(product, tile_of, scale_of)
        received.append(lax.all_to_all(outgoing, "dev", split_axis=0, concat_axis=0, tiled=True))
    exported = jnp.concatenate(received, axis=1)
    return exported.reshape(1, 1, slots, PB, CB)


def solution(mesh):
    placed = (P(None, "dev"), P("grp"), P("grp", "dev"), P("grp", "dev", None, None))
    return jax.shard_map(
        body,
        mesh=mesh,
        in_specs=placed,
        out_specs=P("grp", "dev", None, None, None),
        check_vma=False,
    )
```

```python
import functools

import jax
import jax.numpy as jnp
from jax import lax
from jax.experimental import pallas as pl
from jax.experimental.pallas import tpu as pltpu
from jax.sharding import PartitionSpec as P

PB = 256
CB = 128
W = 128
CHUNKS = PB // W
PANELS = 4
C = PANELS * W
NAUX = 9000
HALF = 4608
QUART = HALF // 4
SIXT = QUART // 4
X, Y = 4, 4
N_DEV = 2 * X * Y
N_GRP = 4
PIECE = SIXT // N_GRP
SPREAD = 8
FILLED = NAUX // PIECE


def dev_id(x, y, core):
    return ((x % X) * Y + (y % Y)) * 2 + core


def ring_pairs(first, shift):
    pairs = []
    for x in range(X):
        for y in range(Y):
            for core in range(2):
                along_x = first == (core == 0)
                dx, dy = (shift, 0) if along_x else (0, shift)
                pairs.append((dev_id(x, y, core), dev_id(x + dx, y + dy, core)))
    return pairs


CORE_PAIRS = [(d, d ^ 1) for d in range(2 * X * Y)]


def move(value, first, shift):
    return lax.ppermute(value, "dev", ring_pairs(first, shift))


def swap(value):
    return lax.ppermute(value, "dev", CORE_PAIRS)


def piece_blocks(z):
    base = []
    for d in range(N_DEV):
        x, y, core = d // (2 * Y), (d // 2) % Y, d % 2
        a, b = (x, y) if core == 0 else (y, x)
        base.append(((core * 4 + a) * 4 + b) * N_GRP)
    return jnp.asarray(base, jnp.int32) + z


def spread_kernel(block_ref, *refs):
    ins, out_ref = refs[:SPREAD], refs[SPREAD]
    for i in range(SPREAD):
        rows = ins[i][...]
        held = block_ref[pl.program_id(0) * SPREAD + i] < FILLED
        out_ref[i] = jnp.where(held, rows, jnp.zeros_like(rows))


def spread(factors, blocks):
    def in_map(i, s, block_ref):
        return (jnp.minimum(block_ref[s * SPREAD + i], FILLED - 1), 0)

    cols = PANELS * PB
    return pl.pallas_call(
        spread_kernel,
        grid_spec=pltpu.PrefetchScalarGridSpec(
            num_scalar_prefetch=1,
            grid=(N_DEV // SPREAD,),
            in_specs=[pl.BlockSpec((PIECE, cols), functools.partial(in_map, i)) for i in range(SPREAD)],
            out_specs=pl.BlockSpec((SPREAD, PIECE, cols), lambda s, block_ref: (s, 0, 0)),
        ),
        out_shape=jax.ShapeDtypeStruct((N_DEV, PIECE, cols), jnp.bfloat16),
        compiler_params=pltpu.CompilerParams(vmem_limit_bytes=32 << 20),
        cost_estimate=pl.CostEstimate(flops=0, bytes_accessed=4 * N_DEV * PIECE * cols, transcendentals=0),
        name="spread_rows",
    )(blocks, *([factors] * SPREAD))


def choose_kernel(panel_ref, *refs):
    ins, out_ref = refs[:-1], refs[-1]
    for i, in_ref in enumerate(ins):
        for h in range(CHUNKS):
            first = h * C + (i % PANELS) * W
            out_ref[i // PANELS, :, first : first + W] = in_ref[0, :, h * W : (h + 1) * W]


def choose(scattered, window):
    count = N_GRP * PANELS

    def in_map(i, s, panel_ref):
        return (panel_ref[i] // 4, 0, panel_ref[i] % 4)

    return pl.pallas_call(
        choose_kernel,
        grid_spec=pltpu.PrefetchScalarGridSpec(
            num_scalar_prefetch=1,
            grid=(1,),
            in_specs=[pl.BlockSpec((1, PIECE, PB), functools.partial(in_map, i)) for i in range(count)],
            out_specs=pl.BlockSpec((N_GRP, PIECE, CHUNKS * C), lambda s, panel_ref: (0, 0, 0)),
        ),
        out_shape=jax.ShapeDtypeStruct((N_GRP, PIECE, CHUNKS * C), jnp.bfloat16),
        compiler_params=pltpu.CompilerParams(vmem_limit_bytes=32 << 20),
        cost_estimate=pl.CostEstimate(flops=0, bytes_accessed=4 * count * PIECE * PB, transcendentals=0),
        name="choose_panels",
    )(window, *([scattered] * count))


def multiply_kernel(count, rows, more, slots, *refs):
    place_ref, refs = refs[0], refs[1:]
    if slots:
        (tile_ref, scale_ref), refs = refs[:2], refs[2:]
    values, factor_ref, refs = refs[:count], refs[count], refs[count + 1 :]
    before_ref, refs = (refs[0], refs[1:]) if more else (None, refs)
    out_ref, total_ref = (refs[0], refs[1]) if slots else (refs[0], refs[0])
    step = pl.program_id(0)
    last = NAUX // rows

    @pl.when(step == 0)
    def _():
        total_ref[...] = before_ref[...] if more else jnp.zeros_like(total_ref)

    def add(value, factor):
        total_ref[...] += lax.dot_general(value, factor, (((0,), (0,)), ((), ())), preferred_element_type=jnp.float32)

    for i in range(count):

        @pl.when(jnp.logical_and(step == i, place_ref[i] != last))
        def _(i=i):
            add(values[i][...], factor_ref[...])

        @pl.when(jnp.logical_and(step == i, place_ref[i] == last))
        def _(i=i):
            left = NAUX - last * rows
            add(values[i][:left], factor_ref[:left])

    if slots:

        @pl.when(step == count - 1)
        def _():
            def slot(s, carry):
                t = tile_ref[s]
                row = pl.multiple_of((t // 8) * W, W)
                col = pl.multiple_of((t % 8) * CB, CB)
                block = total_ref[pl.ds(row, W), pl.ds(col, CB)]
                out_ref[s] = (block * scale_ref[s]).astype(jnp.bfloat16)
                return carry

            lax.fori_loop(0, slots, slot, 0)


def multiply(total, values, places, factors, table=None):
    count, rows, cols = len(values), values[0].shape[0], factors.shape[1]
    more, slots = total is not None, 0 if table is None else table[0].shape[0]
    places = jnp.stack([jnp.asarray(p, jnp.int32) for p in places])
    whole = pl.BlockSpec((C, cols), lambda s, place_ref: (0, 0))
    in_specs, operands = [], []
    if slots:
        in_specs += [pl.BlockSpec(memory_space=pltpu.SMEM)] * 2
        operands += list(table)
    in_specs += [pl.BlockSpec((rows, C), lambda s, place_ref: (0, 0))] * count
    in_specs += [pl.BlockSpec((rows, cols), lambda s, place_ref: (place_ref[s], 0))]
    operands += [*values, factors]
    if more:
        in_specs.append(whole)
        operands.append(total)
    if slots:
        out_spec = pl.BlockSpec((slots, W, CB), lambda s, place_ref: (0, 0, 0))
        out_shape = jax.ShapeDtypeStruct((slots, W, CB), jnp.bfloat16)
    else:
        out_spec, out_shape = whole, jax.ShapeDtypeStruct((C, cols), jnp.float32)
    return pl.pallas_call(
        functools.partial(multiply_kernel, count, rows, more, slots),
        grid_spec=pltpu.PrefetchScalarGridSpec(
            num_scalar_prefetch=1,
            grid=(count,),
            in_specs=in_specs,
            out_specs=out_spec,
            scratch_shapes=[pltpu.VMEM((C, cols), jnp.float32)] if slots else [],
        ),
        out_shape=out_shape,
        compiler_params=pltpu.CompilerParams(vmem_limit_bytes=44 << 20),
        cost_estimate=pl.CostEstimate(
            flops=2 * count * rows * C * cols, bytes_accessed=2 * count * rows * (C + cols) + 8 * C * cols, transcendentals=0
        ),
        name="multiply_slots" if slots else "multiply",
    )(places, *operands)


def gather_ring(piece, first):
    half = piece.shape[0] // 2
    from_behind = move(piece, first, 1)
    from_ahead = move(piece, first, -1)
    low = move(from_behind[:half], first, 1)
    high = move(from_ahead[half:], first, -1)
    return from_behind, from_ahead, low, high


def place_kernel(at_ref, *refs):
    ins, outs = refs[:-CHUNKS], refs[-CHUNKS:]
    for i, in_ref in enumerate(ins):
        start = pl.multiple_of(at_ref[i] * (SIXT // 2), SIXT // 2)
        for h in range(CHUNKS):
            outs[h][pl.ds(start, in_ref.shape[0]), :] = in_ref[:, h * C : (h + 1) * C]


def place(pieces, starts):
    vmem = pl.BlockSpec(memory_space=pltpu.VMEM)
    return pl.pallas_call(
        place_kernel,
        in_specs=[pl.BlockSpec(memory_space=pltpu.SMEM)] + [vmem] * len(pieces),
        out_specs=[vmem] * CHUNKS,
        out_shape=[jax.ShapeDtypeStruct((QUART, C), jnp.bfloat16)] * CHUNKS,
        compiler_params=pltpu.CompilerParams(vmem_limit_bytes=32 << 20),
        cost_estimate=pl.CostEstimate(flops=0, bytes_accessed=4 * QUART * C * CHUNKS, transcendentals=0),
        name="place_pieces",
    )(jnp.stack(starts).astype(jnp.int32), *pieces)


def slot_table(owners, slots, kept):
    count = owners.shape[0]
    same_owner = owners[:, None] == owners[None, :]
    earlier = jnp.arange(count)[None, :] < jnp.arange(count)[:, None]
    ranks = jnp.sum((same_owner & earlier).astype(jnp.int32), axis=-1)
    hit = (owners * 2 + ranks)[None, :] == jnp.arange(slots)[:, None]
    tile_of = jnp.sum(jnp.where(hit, jnp.arange(count)[None, :], 0), axis=1).astype(jnp.int32)
    scale_of = jnp.sum(jnp.where(hit, kept[None, :], 0), axis=1).astype(jnp.float32)
    return tile_of, scale_of


def body(fitted_factors, panel_blocks, kept_tiles, tile_owner):
    me, z = lax.axis_index("dev"), lax.axis_index("grp")
    core = me % 2
    mx, my = me // (2 * Y), (me // 2) % Y
    here_a, here_b = jnp.where(core == 0, mx, my), jnp.where(core == 0, my, mx)
    window = lax.all_gather(panel_blocks, "grp", tiled=True)

    slots = 2 * N_DEV
    table = slot_table(tile_owner[0, 0, :, 0], slots, kept_tiles.reshape(-1))
    leaving = spread(fitted_factors, piece_blocks(z))
    scattered = lax.all_to_all(leaving, "dev", split_axis=0, concat_axis=0, tiled=True)
    chosen = choose(scattered, window)
    sixteenth = lax.all_to_all(chosen, "grp", split_axis=0, concat_axis=0, tiled=True).reshape(SIXT, CHUNKS * C)
    from_behind, from_ahead, low, high = gather_ring(sixteenth, False)
    far = ((here_b + 2) % 4) * 2
    quarts = place(
        [sixteenth, from_behind, from_ahead, low, high],
        [here_b * 2, ((here_b + 3) % 4) * 2, ((here_b + 1) % 4) * 2, far, far + 1],
    )

    def slice_of(core_of, a_of):
        return core_of * 4 + a_of % 4

    received, done = [], None
    for quart in quarts:
        if done is not None:
            quart, done = lax.optimization_barrier((quart, done))
        from_behind, from_ahead, low, high = gather_ring(quart, True)
        done = from_behind
        near, places = [], []
        for value, step in ((quart, 0), (from_behind, 3), (from_ahead, 1)):
            near += [value, swap(value)]
            places += [slice_of(core, here_a + step), slice_of(1 - core, here_b + step)]
        total = multiply(None, near, places, fitted_factors)
        across, others = slice_of(core, here_a + 2) * 2, slice_of(1 - core, here_b + 2) * 2
        outgoing = multiply(
            total, [low, high, swap(low), swap(high)], [across, across + 1, others, others + 1], fitted_factors, table
        )
        received.append(lax.all_to_all(outgoing, "dev", split_axis=0, concat_axis=0, tiled=True))
    exported = jnp.concatenate(received, axis=1)
    return exported.reshape(1, 1, slots, PB, CB)


def solution(mesh):
    placed = (P(None, "dev"), P("grp"), P("grp", "dev"), P("grp", "dev", None, None))
    return jax.shard_map(
        body,
        mesh=mesh,
        in_specs=placed,
        out_specs=P("grp", "dev", None, None, None),
        check_vma=False,
    )
```

```python
import functools

import jax
import jax.numpy as jnp
from jax import lax
from jax.experimental import pallas as pl
from jax.experimental.pallas import tpu as pltpu
from jax.sharding import PartitionSpec as P

PB = 256
CB = 128
W = 128
CHUNKS = PB // W
PANELS = 4
C = PANELS * W
NAUX = 9000
HALF = 4608
QUART = HALF // 4
SIXT = QUART // 4
X, Y = 4, 4
N_DEV = 2 * X * Y
N_GRP = 4
PIECE = SIXT // N_GRP
SPREAD = 8
FILLED = NAUX // PIECE


def dev_id(x, y, core):
    return ((x % X) * Y + (y % Y)) * 2 + core


def ring_pairs(first, shift):
    pairs = []
    for x in range(X):
        for y in range(Y):
            for core in range(2):
                along_x = first == (core == 0)
                dx, dy = (shift, 0) if along_x else (0, shift)
                pairs.append((dev_id(x, y, core), dev_id(x + dx, y + dy, core)))
    return pairs


CORE_PAIRS = [(d, d ^ 1) for d in range(2 * X * Y)]


def move(value, first, shift):
    return lax.ppermute(value, "dev", ring_pairs(first, shift))


def move_group(value, shift):
    return lax.ppermute(value, "grp", [(g, (g + shift) % N_GRP) for g in range(N_GRP)])


def swap(value):
    return lax.ppermute(value, "dev", CORE_PAIRS)


def piece_blocks(z):
    base = []
    for d in range(N_DEV):
        x, y, core = d // (2 * Y), (d // 2) % Y, d % 2
        a, b = (x, y) if core == 0 else (y, x)
        base.append(((core * 4 + a) * 4 + b) * N_GRP)
    return jnp.asarray(base, jnp.int32) + z


def spread_kernel(width, block_ref, slot_ref, *refs):
    ins, out_ref = refs[:-1], refs[-1]
    for i in range(SPREAD):
        held = block_ref[pl.program_id(0) * SPREAD + i] < FILLED
        for s in range(width):
            rows = ins[i * width + s][...]
            out_ref[i, :, s * PB : (s + 1) * PB] = jnp.where(held, rows, jnp.zeros_like(rows))


def spread(factors, blocks, panel_in):
    width = panel_in.shape[0]

    def in_map(i, s, step, block_ref, panel_ref):
        return (jnp.minimum(block_ref[step * SPREAD + i], FILLED - 1), panel_ref[s])

    cols = width * PB
    return pl.pallas_call(
        functools.partial(spread_kernel, width),
        grid_spec=pltpu.PrefetchScalarGridSpec(
            num_scalar_prefetch=2,
            grid=(N_DEV // SPREAD,),
            in_specs=[
                pl.BlockSpec((PIECE, PB), functools.partial(in_map, i, s)) for i in range(SPREAD) for s in range(width)
            ],
            out_specs=pl.BlockSpec((SPREAD, PIECE, cols), lambda step, block_ref, panel_ref: (step, 0, 0)),
        ),
        out_shape=jax.ShapeDtypeStruct((N_DEV, PIECE, cols), jnp.bfloat16),
        compiler_params=pltpu.CompilerParams(vmem_limit_bytes=32 << 20),
        cost_estimate=pl.CostEstimate(flops=0, bytes_accessed=4 * N_DEV * PIECE * cols, transcendentals=0),
        name="spread_rows",
    )(blocks, panel_in, *([factors] * (SPREAD * width)))


def choose_kernel(source_ref, slot_ref, *refs):
    ins, outs = refs[:-N_GRP], refs[-N_GRP:]
    for i, in_ref in enumerate(ins):
        for h in range(CHUNKS):
            first = h * C + (i % PANELS) * W
            outs[i // PANELS][:, first : first + W] = in_ref[0, :, h * W : (h + 1) * W]


def choose(scattered, source, slot):
    count = N_GRP * PANELS

    def in_map(i, s, source_ref, slot_ref):
        return (source_ref[i], 0, slot_ref[i])

    return pl.pallas_call(
        choose_kernel,
        grid_spec=pltpu.PrefetchScalarGridSpec(
            num_scalar_prefetch=2,
            grid=(1,),
            in_specs=[pl.BlockSpec((1, PIECE, PB), functools.partial(in_map, i)) for i in range(count)],
            out_specs=[pl.BlockSpec((PIECE, CHUNKS * C), lambda s, source_ref, slot_ref: (0, 0))] * N_GRP,
        ),
        out_shape=[jax.ShapeDtypeStruct((PIECE, CHUNKS * C), jnp.bfloat16)] * N_GRP,
        compiler_params=pltpu.CompilerParams(vmem_limit_bytes=32 << 20),
        cost_estimate=pl.CostEstimate(flops=0, bytes_accessed=4 * count * PIECE * PB, transcendentals=0),
        name="choose_panels",
    )(source, slot, *([scattered] * count))


def join_kernel(z_ref, *refs):
    ins, outs = refs[:-CHUNKS], refs[-CHUNKS:]
    for shift, in_ref in enumerate(ins):
        at = lax.rem(z_ref[0] + N_GRP - shift, N_GRP)
        for h in range(CHUNKS):
            outs[h][at] = in_ref[:, h * C : (h + 1) * C]


def join(pieces, z):
    chunks = pl.pallas_call(
        join_kernel,
        grid_spec=pltpu.PrefetchScalarGridSpec(
            num_scalar_prefetch=1,
            grid=(1,),
            in_specs=[pl.BlockSpec((PIECE, CHUNKS * C), lambda s, z_ref: (0, 0))] * N_GRP,
            out_specs=[pl.BlockSpec((N_GRP, PIECE, C), lambda s, z_ref: (0, 0, 0))] * CHUNKS,
        ),
        out_shape=[jax.ShapeDtypeStruct((N_GRP, PIECE, C), jnp.bfloat16)] * CHUNKS,
        compiler_params=pltpu.CompilerParams(vmem_limit_bytes=32 << 20),
        cost_estimate=pl.CostEstimate(flops=0, bytes_accessed=4 * SIXT * CHUNKS * C, transcendentals=0),
        name="join_groups",
    )(z.reshape(1), *pieces)
    return [chunk.reshape(SIXT, C) for chunk in chunks]


def gather_window(panel_blocks, z):
    shape = (N_GRP, PANELS)
    mine = jnp.arange(N_GRP)[:, None]
    window = jnp.where(mine == z, panel_blocks[None, :], jnp.zeros(shape, jnp.int32))
    for shift in range(1, N_GRP):
        other = move_group(panel_blocks, shift)
        window = jnp.where(mine == (z - shift) % N_GRP, other[None, :], window)
    return window.reshape(-1)


def scatter_window(factors, window, me, z):
    panels = jnp.arange(N_DEV * PANELS)
    named = jnp.any(panels[:, None] == window[None, :], axis=1).reshape(N_DEV, PANELS).astype(jnp.int32)
    earlier = jnp.arange(PANELS)[None, :] < jnp.arange(PANELS)[:, None]
    slot = jnp.sum(jnp.where(earlier[None], named[:, None, :], 0), axis=2)
    most = jnp.max(jnp.sum(named, axis=1))
    source = window // PANELS
    hit = window[:, None] == panels[None, :]
    slot_of = jnp.sum(jnp.where(hit, slot.reshape(1, -1), 0), axis=1).astype(jnp.int32)
    own = (jnp.arange(N_DEV) == me)[:, None]
    my_named = jnp.sum(jnp.where(own, named, 0), axis=0)
    my_slot = jnp.sum(jnp.where(own, slot, 0), axis=0)
    fill = (my_named[None, :] == 1) & (my_slot[None, :] == jnp.arange(PANELS)[:, None])
    panel_in = jnp.sum(jnp.where(fill, jnp.arange(PANELS)[None, :], 0), axis=1).astype(jnp.int32)
    blocks = piece_blocks(z)
    turned = jnp.arange(N_GRP * PANELS)[None, :] == ((jnp.arange(N_GRP * PANELS) + z * PANELS) % (N_GRP * PANELS))[:, None]
    source = jnp.sum(jnp.where(turned, source[None, :], 0), axis=1).astype(jnp.int32)
    slot_of = jnp.sum(jnp.where(turned, slot_of[None, :], 0), axis=1).astype(jnp.int32)

    def with_slots(width):
        def run(blocks, panel_in, source, slot_of):
            leaving = spread(factors, blocks, panel_in[:width])
            scattered = lax.all_to_all(leaving, "dev", split_axis=0, concat_axis=0, tiled=True)
            return choose(scattered, source, slot_of)

        return run

    branches = [with_slots(width) for width in range(1, PANELS + 1)]
    return lax.switch(most - 1, branches, blocks, panel_in, source, slot_of)


def multiply_kernel(count, more, slots, *refs):
    place_ref, refs = refs[0], refs[1:]
    if slots:
        (tile_ref, scale_ref), refs = refs[:2], refs[2:]
    values, factor_ref, refs = refs[: CHUNKS * count], refs[CHUNKS * count], refs[CHUNKS * count + 1 :]
    before_ref, refs = (refs[0], refs[1:]) if more else (None, refs)
    out_ref, refs = refs[0], refs[1:]
    total_ref, refs = (refs[0], refs[1:]) if slots else (out_ref, refs)
    held_ref, sems = refs
    step = pl.program_id(0)
    last = NAUX // QUART
    copies = [pltpu.make_async_copy(values[i], held_ref.at[i], sems.at[i]) for i in range(CHUNKS * count)]

    @pl.when(step == 0)
    def _():
        for copy in copies:
            copy.start()

    def add(i, rows):
        for h in range(CHUNKS):
            copies[CHUNKS * i + h].wait()
            part = lax.dot_general(
                held_ref[CHUNKS * i + h, :rows],
                factor_ref[:rows],
                (((0,), (0,)), ((), ())),
                preferred_element_type=jnp.float32,
            )
            if i > 0:
                part += total_ref[h]
            elif more:
                part += before_ref[h]
            total_ref[h] = part

    for i in range(count):

        @pl.when(jnp.logical_and(step == i, place_ref[i] != last))
        def _(i=i):
            add(i, QUART)

        @pl.when(jnp.logical_and(step == i, place_ref[i] == last))
        def _(i=i):
            add(i, NAUX - last * QUART)

    if slots:

        @pl.when(step == count - 1)
        def _():
            def slot(s, carry):
                t = tile_ref[s]
                row = pl.multiple_of((t // 8) * W, W)
                col = pl.multiple_of((t % 8) * CB, CB)
                for h in range(CHUNKS):
                    block = total_ref[h, pl.ds(row, W), pl.ds(col, CB)]
                    out_ref[s, h * W : (h + 1) * W, :] = (block * scale_ref[s]).astype(jnp.bfloat16)
                return carry

            lax.fori_loop(0, slots, slot, 0, unroll=4)


def multiply(total, values, places, factors, table=None):
    count, cols = len(values), factors.shape[1]
    more, slots = total is not None, 0 if table is None else table[0].shape[0]
    places = jnp.stack([jnp.asarray(p, jnp.int32) for p in places])
    vmem = pl.BlockSpec(memory_space=pltpu.VMEM)
    in_specs, operands = [], []
    if slots:
        in_specs += [pl.BlockSpec(memory_space=pltpu.SMEM)] * 2
        operands += list(table)
    in_specs += [pl.BlockSpec(memory_space=pl.ANY)] * (CHUNKS * count)
    in_specs += [pl.BlockSpec((QUART, cols), lambda s, place_ref: (place_ref[s], 0))]
    operands += [array for value in values for array in value]
    operands.append(factors)
    if more:
        in_specs.append(vmem)
        operands.append(total)
    if slots:
        out_shape = jax.ShapeDtypeStruct((slots, PB, CB), jnp.bfloat16)
    else:
        out_shape = jax.ShapeDtypeStruct((CHUNKS, C, cols), jnp.float32)
    scratch = [pltpu.VMEM((CHUNKS, C, cols), jnp.float32)] if slots else []
    scratch += [pltpu.VMEM((CHUNKS * count, QUART, C), jnp.bfloat16), pltpu.SemaphoreType.DMA((CHUNKS * count,))]
    moved = 2 * count * QUART * (CHUNKS * C + cols) + 8 * CHUNKS * C * cols
    return pl.pallas_call(
        functools.partial(multiply_kernel, count, more, slots),
        grid_spec=pltpu.PrefetchScalarGridSpec(
            num_scalar_prefetch=1, grid=(count,), in_specs=in_specs, out_specs=vmem, scratch_shapes=scratch
        ),
        out_shape=out_shape,
        input_output_aliases={len(operands): 0} if more and not slots else {},
        compiler_params=pltpu.CompilerParams(vmem_limit_bytes=40 << 20),
        cost_estimate=pl.CostEstimate(
            flops=2 * count * QUART * CHUNKS * C * cols, bytes_accessed=moved, transcendentals=0
        ),
        name="multiply_slots" if slots else "multiply",
    )(places, *operands)


def place_kernel(at_ref, *refs):
    ins, outs = refs[:-CHUNKS], refs[-CHUNKS:]
    for i, in_ref in enumerate(ins):
        start = pl.multiple_of(at_ref[i // CHUNKS] * SIXT, SIXT)
        outs[i % CHUNKS][pl.ds(start, SIXT), :] = in_ref[...]


def place(pieces, places):
    arrays = [array for piece in pieces for array in piece]
    whole = pl.BlockSpec((QUART, C), lambda s, at_ref: (0, 0))
    return pl.pallas_call(
        place_kernel,
        grid_spec=pltpu.PrefetchScalarGridSpec(
            num_scalar_prefetch=1,
            grid=(1,),
            in_specs=[pl.BlockSpec((SIXT, C), lambda s, at_ref: (0, 0))] * len(arrays),
            out_specs=[whole] * CHUNKS,
        ),
        out_shape=[jax.ShapeDtypeStruct((QUART, C), jnp.bfloat16)] * CHUNKS,
        compiler_params=pltpu.CompilerParams(vmem_limit_bytes=32 << 20),
        cost_estimate=pl.CostEstimate(flops=0, bytes_accessed=4 * QUART * C * CHUNKS, transcendentals=0),
        name="place_pieces",
    )(jnp.stack(places).astype(jnp.int32), *arrays)


def slot_table(owners, slots, kept):
    count = owners.shape[0]
    same_owner = owners[:, None] == owners[None, :]
    earlier = jnp.arange(count)[None, :] < jnp.arange(count)[:, None]
    ranks = jnp.sum((same_owner & earlier).astype(jnp.int32), axis=-1)
    hit = (owners * 2 + ranks)[None, :] == jnp.arange(slots)[:, None]
    tile_of = jnp.sum(jnp.where(hit, jnp.arange(count)[None, :], 0), axis=1).astype(jnp.int32)
    scale_of = jnp.sum(jnp.where(hit, kept[None, :], 0), axis=1).astype(jnp.float32)
    return tile_of, scale_of


def body(fitted_factors, panel_blocks, kept_tiles, tile_owner):
    me, z = lax.axis_index("dev"), lax.axis_index("grp")
    core = me % 2
    mx, my = me // (2 * Y), (me // 2) % Y
    here_a, here_b = jnp.where(core == 0, mx, my), jnp.where(core == 0, my, mx)
    window = gather_window(panel_blocks, z)

    slots = 2 * N_DEV
    table = slot_table(tile_owner[0, 0, :, 0], slots, kept_tiles.reshape(-1))
    chosen = scatter_window(fitted_factors, window, me, z)
    pieces = [chosen[0]] + [move_group(chosen[shift], shift) for shift in range(1, N_GRP)]
    sixteenth = join(pieces, z)
    first, second = sixteenth
    behind_first, ahead_second = move(first, False, 1), move(second, False, -1)
    ahead_first, behind_second = move(first, False, -1), move(second, False, 1)
    across_first, across_second = move(behind_first, False, 1), move(ahead_second, False, -1)
    quarts = place(
        [
            (first, second),
            (behind_first, behind_second),
            (ahead_first, ahead_second),
            (across_first, across_second),
        ],
        [here_b, (here_b + 3) % 4, (here_b + 1) % 4, (here_b + 2) % 4],
    )

    def slice_of(core_of, a_of):
        return core_of * 4 + a_of % 4

    def both(value):
        return tuple(swap(array) for array in value)

    def near(total, value, step):
        return multiply(total, [value], [slice_of(core, here_a + step)], fitted_factors)

    def other(total, value, step):
        return multiply(total, [value], [slice_of(1 - core, here_b + step)], fitted_factors)

    first, second = quarts
    behind_first, ahead_second = move(first, True, 1), move(second, True, -1)
    ahead_first, behind_second = move(first, True, -1), move(second, True, 1)
    swapped = both((first, second))
    total = near(None, (first, second), 0)
    behind_first, ahead_second, total = lax.optimization_barrier((behind_first, ahead_second, total))
    across = (move(behind_first, True, 1), move(ahead_second, True, -1))
    half = both((behind_first, ahead_second))
    total = other(total, swapped, 0)
    behind_second, ahead_first, total = lax.optimization_barrier((behind_second, ahead_first, total))
    behind, ahead = (behind_first, behind_second), (ahead_first, ahead_second)
    rest = both((behind_second, ahead_first))
    total = multiply(total, [behind, ahead], [slice_of(core, here_a + 3), slice_of(core, here_a + 1)], fitted_factors)
    across, total = lax.optimization_barrier((across, total))
    swapped = both(across)
    total = multiply(
        total,
        [(half[0], rest[0]), (rest[1], half[1])],
        [slice_of(1 - core, here_b + 3), slice_of(1 - core, here_b + 1)],
        fitted_factors,
    )
    outgoing = multiply(
        total,
        [across, swapped],
        [slice_of(core, here_a + 2), slice_of(1 - core, here_b + 2)],
        fitted_factors,
        table,
    )
    exported = lax.all_to_all(outgoing, "dev", split_axis=0, concat_axis=0, tiled=True)
    return exported.reshape(1, 1, slots, PB, CB)


def solution(mesh):
    placed = (P(None, "dev"), P("grp"), P("grp", "dev"), P("grp", "dev", None, None))
    return jax.shard_map(
        body,
        mesh=mesh,
        in_specs=placed,
        out_specs=P("grp", "dev", None, None, None),
        check_vma=False,
    )
```

```python
import functools

import jax
import jax.numpy as jnp
from jax import lax
from jax.experimental import pallas as pl
from jax.experimental.pallas import tpu as pltpu
from jax.sharding import PartitionSpec as P

PB = 256
CB = 128
W = 128
CHUNKS = PB // W
PANELS = 4
C = PANELS * W
NAUX = 9000
HALF = 4608
QUART = HALF // 4
SIXT = QUART // 4
X, Y = 4, 4
N_DEV = 2 * X * Y
N_GRP = 4
PIECE = SIXT // N_GRP
SPREAD = 8
FILLED = NAUX // PIECE


def dev_id(x, y, core):
    return ((x % X) * Y + (y % Y)) * 2 + core


def ring_pairs(first, shift):
    pairs = []
    for x in range(X):
        for y in range(Y):
            for core in range(2):
                along_x = first == (core == 0)
                dx, dy = (shift, 0) if along_x else (0, shift)
                pairs.append((dev_id(x, y, core), dev_id(x + dx, y + dy, core)))
    return pairs


CORE_PAIRS = [(d, d ^ 1) for d in range(2 * X * Y)]


def move(value, first, shift):
    return lax.ppermute(value, "dev", ring_pairs(first, shift))


def move_group(value, shift):
    return lax.ppermute(value, "grp", [(g, (g + shift) % N_GRP) for g in range(N_GRP)])


def swap(value):
    return lax.ppermute(value, "dev", CORE_PAIRS)


def piece_blocks(z):
    base = []
    for d in range(N_DEV):
        x, y, core = d // (2 * Y), (d // 2) % Y, d % 2
        a, b = (x, y) if core == 0 else (y, x)
        base.append(((core * 4 + a) * 4 + b) * N_GRP)
    return jnp.asarray(base, jnp.int32) + z


def spread_kernel(width, block_ref, slot_ref, *refs):
    ins, out_ref = refs[:-1], refs[-1]
    for i in range(SPREAD):
        held = block_ref[pl.program_id(0) * SPREAD + i] < FILLED
        for s in range(width):
            rows = ins[i * width + s][...]
            out_ref[i, :, s * PB : (s + 1) * PB] = jnp.where(held, rows, jnp.zeros_like(rows))


def spread(factors, blocks, panel_in):
    width = panel_in.shape[0]

    def in_map(i, s, step, block_ref, panel_ref):
        return (jnp.minimum(block_ref[step * SPREAD + i], FILLED - 1), panel_ref[s])

    cols = width * PB
    return pl.pallas_call(
        functools.partial(spread_kernel, width),
        grid_spec=pltpu.PrefetchScalarGridSpec(
            num_scalar_prefetch=2,
            grid=(N_DEV // SPREAD,),
            in_specs=[
                pl.BlockSpec((PIECE, PB), functools.partial(in_map, i, s)) for i in range(SPREAD) for s in range(width)
            ],
            out_specs=pl.BlockSpec((SPREAD, PIECE, cols), lambda step, block_ref, panel_ref: (step, 0, 0)),
        ),
        out_shape=jax.ShapeDtypeStruct((N_DEV, PIECE, cols), jnp.bfloat16),
        compiler_params=pltpu.CompilerParams(vmem_limit_bytes=32 << 20),
        cost_estimate=pl.CostEstimate(flops=0, bytes_accessed=4 * N_DEV * PIECE * cols, transcendentals=0),
        name="spread_rows",
    )(blocks, panel_in, *([factors] * (SPREAD * width)))


def choose_kernel(source_ref, slot_ref, *refs):
    ins, outs = refs[:-N_GRP], refs[-N_GRP:]
    for i, in_ref in enumerate(ins):
        for h in range(CHUNKS):
            first = h * C + (i % PANELS) * W
            outs[i // PANELS][:, first : first + W] = in_ref[0, :, h * W : (h + 1) * W]


def choose(scattered, source, slot):
    count = N_GRP * PANELS

    def in_map(i, s, source_ref, slot_ref):
        return (source_ref[i], 0, slot_ref[i])

    return pl.pallas_call(
        choose_kernel,
        grid_spec=pltpu.PrefetchScalarGridSpec(
            num_scalar_prefetch=2,
            grid=(1,),
            in_specs=[pl.BlockSpec((1, PIECE, PB), functools.partial(in_map, i)) for i in range(count)],
            out_specs=[pl.BlockSpec((PIECE, CHUNKS * C), lambda s, source_ref, slot_ref: (0, 0))] * N_GRP,
        ),
        out_shape=[jax.ShapeDtypeStruct((PIECE, CHUNKS * C), jnp.bfloat16)] * N_GRP,
        compiler_params=pltpu.CompilerParams(vmem_limit_bytes=32 << 20),
        cost_estimate=pl.CostEstimate(flops=0, bytes_accessed=4 * count * PIECE * PB, transcendentals=0),
        name="choose_panels",
    )(source, slot, *([scattered] * count))


def join_kernel(z_ref, *refs):
    ins, outs = refs[:-CHUNKS], refs[-CHUNKS:]
    for shift, in_ref in enumerate(ins):
        at = lax.rem(z_ref[0] + N_GRP - shift, N_GRP)
        for h in range(CHUNKS):
            outs[h][at] = in_ref[:, h * C : (h + 1) * C]


def join(pieces, z):
    chunks = pl.pallas_call(
        join_kernel,
        grid_spec=pltpu.PrefetchScalarGridSpec(
            num_scalar_prefetch=1,
            grid=(1,),
            in_specs=[pl.BlockSpec((PIECE, CHUNKS * C), lambda s, z_ref: (0, 0))] * N_GRP,
            out_specs=[pl.BlockSpec((N_GRP, PIECE, C), lambda s, z_ref: (0, 0, 0))] * CHUNKS,
        ),
        out_shape=[jax.ShapeDtypeStruct((N_GRP, PIECE, C), jnp.bfloat16)] * CHUNKS,
        compiler_params=pltpu.CompilerParams(vmem_limit_bytes=32 << 20),
        cost_estimate=pl.CostEstimate(flops=0, bytes_accessed=4 * SIXT * CHUNKS * C, transcendentals=0),
        name="join_groups",
    )(z.reshape(1), *pieces)
    return [chunk.reshape(SIXT, C) for chunk in chunks]


def gather_window(panel_blocks, z):
    shape = (N_GRP, PANELS)
    mine = jnp.arange(N_GRP)[:, None]
    window = jnp.where(mine == z, panel_blocks[None, :], jnp.zeros(shape, jnp.int32))
    for shift in range(1, N_GRP):
        other = move_group(panel_blocks, shift)
        window = jnp.where(mine == (z - shift) % N_GRP, other[None, :], window)
    return window.reshape(-1)


def scatter_window(factors, window, me, z):
    panels = jnp.arange(N_DEV * PANELS)
    named = jnp.any(panels[:, None] == window[None, :], axis=1).reshape(N_DEV, PANELS).astype(jnp.int32)
    earlier = jnp.arange(PANELS)[None, :] < jnp.arange(PANELS)[:, None]
    slot = jnp.sum(jnp.where(earlier[None], named[:, None, :], 0), axis=2)
    most = jnp.max(jnp.sum(named, axis=1))
    source = window // PANELS
    hit = window[:, None] == panels[None, :]
    slot_of = jnp.sum(jnp.where(hit, slot.reshape(1, -1), 0), axis=1).astype(jnp.int32)
    own = (jnp.arange(N_DEV) == me)[:, None]
    my_named = jnp.sum(jnp.where(own, named, 0), axis=0)
    my_slot = jnp.sum(jnp.where(own, slot, 0), axis=0)
    fill = (my_named[None, :] == 1) & (my_slot[None, :] == jnp.arange(PANELS)[:, None])
    panel_in = jnp.sum(jnp.where(fill, jnp.arange(PANELS)[None, :], 0), axis=1).astype(jnp.int32)
    blocks = piece_blocks(z)
    turned = jnp.arange(N_GRP * PANELS)[None, :] == ((jnp.arange(N_GRP * PANELS) + z * PANELS) % (N_GRP * PANELS))[:, None]
    source = jnp.sum(jnp.where(turned, source[None, :], 0), axis=1).astype(jnp.int32)
    slot_of = jnp.sum(jnp.where(turned, slot_of[None, :], 0), axis=1).astype(jnp.int32)

    def with_slots(width):
        def run(blocks, panel_in, source, slot_of):
            leaving = spread(factors, blocks, panel_in[:width])
            scattered = lax.all_to_all(leaving, "dev", split_axis=0, concat_axis=0, tiled=True)
            return choose(scattered, source, slot_of)

        return run

    branches = [with_slots(width) for width in range(1, PANELS + 1)]
    return lax.switch(most - 1, branches, blocks, panel_in, source, slot_of)


def multiply_kernel(items, before, sides, slots, through, *refs):
    place_ref, refs = refs[0], refs[1:]
    if slots:
        (tile_ref, scale_ref), refs = refs[:2], refs[2:]
    count = len(items)
    arrays = max(array for array, _, _ in items) + 1
    values, factor_refs, refs = refs[:arrays], refs[arrays : arrays + sides], refs[arrays + sides :]
    before_refs, refs = refs[:before], refs[before:]
    if slots:
        out_ref, total_refs, refs = refs[0], refs[1 : 1 + CHUNKS], refs[1 + CHUNKS :]
    else:
        total_refs, refs = refs[: CHUNKS * sides], refs[CHUNKS * sides + through :]
    held_ref, sems = refs
    step = pl.program_id(0)
    last = NAUX // QUART
    copies = []
    for i, (array, at, _) in enumerate(items):
        source = values[array] if at is None else values[array].at[at]
        copies.append(pltpu.make_async_copy(source, held_ref.at[i], sems.at[i]))

    @pl.when(step == 0)
    def _():
        for copy in copies:
            copy.start()

    def add(i, rows):
        h = items[i][2]
        for side in range(sides):
            part = lax.dot_general(
                held_ref[i, :rows], factor_refs[side][:rows], (((0,), (0,)), ((), ())), preferred_element_type=jnp.float32
            )
            at = CHUNKS * side + h
            if any(chunk == h for _, _, chunk in items[:i]):
                part += total_refs[at][...]
            else:
                for before_ref in before_refs[at :: CHUNKS * sides]:
                    part += before_ref[...]
            total_refs[at][...] = part

    for i in range(count):

        @pl.when(step == i)
        def _(i=i):
            copies[i].wait()

            @pl.when(place_ref[i] != last)
            def _():
                add(i, QUART)

            @pl.when(place_ref[i] == last)
            def _():
                add(i, NAUX - last * QUART)

    if slots:

        @pl.when(step == count - 1)
        def _():
            def slot(s, carry):
                t = tile_ref[s]
                row = pl.multiple_of((t // 8) * W, W)
                col = pl.multiple_of((t % 8) * CB, CB)
                for h in range(CHUNKS):
                    block = total_refs[h][pl.ds(row, W), pl.ds(col, CB)]
                    out_ref[s, h * W : (h + 1) * W, :] = (block * scale_ref[s]).astype(jnp.bfloat16)
                return carry

            lax.fori_loop(0, slots, slot, 0, unroll=4)


def multiply(before, items, arrays, places, factors, table=None, through=0):
    count, cols, sides = len(items), factors[0].shape[1], len(factors)
    slots = 0 if table is None else table[0].shape[0]
    places = jnp.stack([jnp.asarray(p, jnp.int32) for p in places])
    vmem = pl.BlockSpec(memory_space=pltpu.VMEM)
    in_specs, operands = [], [*arrays, *factors, *before]
    if slots:
        in_specs += [pl.BlockSpec(memory_space=pltpu.SMEM)] * 2
        operands = [*table, *operands]
    in_specs += [pl.BlockSpec(memory_space=pl.ANY)] * len(arrays)
    in_specs += [pl.BlockSpec((QUART, cols), lambda s, place_ref: (place_ref[s], 0))] * sides
    in_specs += [vmem] * len(before)
    aliases = {}
    if slots:
        out_specs, out_shape = vmem, jax.ShapeDtypeStruct((slots, PB, CB), jnp.bfloat16)
    else:
        sums = CHUNKS * sides
        out_specs = [vmem] * sums + [pl.BlockSpec(memory_space=pl.ANY)] * through
        out_shape = [jax.ShapeDtypeStruct((C, cols), jnp.float32)] * sums
        out_shape += [jax.ShapeDtypeStruct(array.shape, array.dtype) for array in arrays[:through]]
        aliases.update({1 + i: sums + i for i in range(through)})
        aliases.update({1 + len(operands) - sums + i: i for i in range(sums) if before})
    scratch = [pltpu.VMEM((C, cols), jnp.float32)] * CHUNKS if slots else []
    scratch += [pltpu.VMEM((count, QUART, C), jnp.bfloat16), pltpu.SemaphoreType.DMA((count,))]
    moved = 2 * count * QUART * (C + sides * cols)
    return pl.pallas_call(
        functools.partial(multiply_kernel, items, len(before), sides, slots, through),
        grid_spec=pltpu.PrefetchScalarGridSpec(
            num_scalar_prefetch=1, grid=(count,), in_specs=in_specs, out_specs=out_specs, scratch_shapes=scratch
        ),
        out_shape=out_shape,
        input_output_aliases=aliases,
        compiler_params=pltpu.CompilerParams(vmem_limit_bytes=(28 if slots else 22) << 20),
        cost_estimate=pl.CostEstimate(flops=2 * count * sides * QUART * C * cols, bytes_accessed=moved, transcendentals=0),
        name="multiply_slots" if slots else "multiply",
    )(places, *operands)


def place_kernel(at_ref, *refs):
    ins, outs = refs[:-CHUNKS], refs[-CHUNKS:]
    for i, in_ref in enumerate(ins):
        start = pl.multiple_of(at_ref[i // CHUNKS] * SIXT, SIXT)
        outs[i % CHUNKS][pl.ds(start, SIXT), :] = in_ref[...]


def place(pieces, places):
    arrays = [array for piece in pieces for array in piece]
    whole = pl.BlockSpec((QUART, C), lambda s, at_ref: (0, 0))
    return pl.pallas_call(
        place_kernel,
        grid_spec=pltpu.PrefetchScalarGridSpec(
            num_scalar_prefetch=1,
            grid=(1,),
            in_specs=[pl.BlockSpec((SIXT, C), lambda s, at_ref: (0, 0))] * len(arrays),
            out_specs=[whole] * CHUNKS,
        ),
        out_shape=[jax.ShapeDtypeStruct((QUART, C), jnp.bfloat16)] * CHUNKS,
        compiler_params=pltpu.CompilerParams(vmem_limit_bytes=32 << 20),
        cost_estimate=pl.CostEstimate(flops=0, bytes_accessed=4 * QUART * C * CHUNKS, transcendentals=0),
        name="place_pieces",
    )(jnp.stack(places).astype(jnp.int32), *arrays)


def slot_table(owners, slots, kept):
    count = owners.shape[0]
    same_owner = owners[:, None] == owners[None, :]
    earlier = jnp.arange(count)[None, :] < jnp.arange(count)[:, None]
    ranks = jnp.sum((same_owner & earlier).astype(jnp.int32), axis=-1)
    hit = (owners * 2 + ranks)[None, :] == jnp.arange(slots)[:, None]
    tile_of = jnp.sum(jnp.where(hit, jnp.arange(count)[None, :], 0), axis=1).astype(jnp.int32)
    scale_of = jnp.sum(jnp.where(hit, kept[None, :], 0), axis=1).astype(jnp.float32)
    return tile_of, scale_of


def body(fitted_factors, panel_blocks, kept_tiles, tile_owner):
    me, z = lax.axis_index("dev"), lax.axis_index("grp")
    core = me % 2
    mx, my = me // (2 * Y), (me // 2) % Y
    here_a, here_b = jnp.where(core == 0, mx, my), jnp.where(core == 0, my, mx)
    window = gather_window(panel_blocks, z)

    slots = 2 * N_DEV
    table = slot_table(tile_owner[0, 0, :, 0], slots, kept_tiles.reshape(-1))
    sibling_factors = swap(fitted_factors)
    chosen = scatter_window(fitted_factors, window, me, z)
    pieces = [chosen[0]] + [move_group(chosen[shift], shift) for shift in range(1, N_GRP)]
    sixteenth = join(pieces, z)
    first, second = sixteenth
    behind_first, ahead_second = move(first, False, 1), move(second, False, -1)
    ahead_first, behind_second = move(first, False, -1), move(second, False, 1)
    across_first, across_second = move(behind_first, False, 1), move(ahead_second, False, -1)
    quarts = place(
        [
            (first, second),
            (behind_first, behind_second),
            (ahead_first, ahead_second),
            (across_first, across_second),
        ],
        [here_b, (here_b + 3) % 4, (here_b + 1) % 4, (here_b + 2) % 4],
    )

    def slice_of(core_of, a_of):
        return core_of * 4 + a_of % 4

    def add(before, arrays, places, factors, table=None, through=0):
        return multiply(before, [(i, None, i % CHUNKS) for i in range(len(arrays))], arrays, places, factors, table, through)

    first, second = quarts
    here, behind, ahead, far = [slice_of(core, here_a + step) for step in (0, 3, 1, 2)]
    other_far = slice_of(1 - core, here_b + 2)
    factors = [fitted_factors, sibling_factors]
    behind_first, ahead_second = move(first, True, 1), move(second, True, -1)
    ahead_first, behind_second = move(first, True, -1), move(second, True, 1)
    sums = add([], [first, second], [here, here], factors)
    *sums, behind_first, ahead_second = add(sums, [behind_first, ahead_second], [behind, ahead], factors, through=2)
    far_first, far_second = move(behind_first, True, 1), move(ahead_second, True, -1)
    sums = add(sums, [ahead_first, behind_second], [ahead, behind], factors)
    own, other = sums[:CHUNKS], sums[CHUNKS:]
    own = add(own, [far_first, far_second], [far, far], factors[:1])
    outgoing = add(
        [*own, *[swap(value) for value in other]],
        [swap(far_first), swap(far_second)],
        [other_far, other_far],
        factors[:1],
        table,
    )
    exported = lax.all_to_all(outgoing, "dev", split_axis=0, concat_axis=0, tiled=True)
    return exported.reshape(1, 1, slots, PB, CB)


def solution(mesh):
    placed = (P(None, "dev"), P("grp"), P("grp", "dev"), P("grp", "dev", None, None))
    return jax.shard_map(
        body,
        mesh=mesh,
        in_specs=placed,
        out_specs=P("grp", "dev", None, None, None),
        check_vma=False,
    )
```

```python
import functools

import jax
import jax.numpy as jnp
from jax import lax
from jax.experimental import pallas as pl
from jax.experimental.pallas import tpu as pltpu
from jax.sharding import PartitionSpec as P

PB = 256
CB = 128
W = 128
CHUNKS = PB // W
PANELS = 4
C = PANELS * W
NAUX = 9000
HALF = 4608
QUART = HALF // 4
SIXT = QUART // 4
X, Y = 4, 4
N_DEV = 2 * X * Y
N_GRP = 4
PIECE = SIXT // N_GRP
SPREAD = 8
FILLED = NAUX // PIECE


def dev_id(x, y, core):
    return ((x % X) * Y + (y % Y)) * 2 + core


def ring_pairs(first, shift):
    pairs = []
    for x in range(X):
        for y in range(Y):
            for core in range(2):
                along_x = first == (core == 0)
                dx, dy = (shift, 0) if along_x else (0, shift)
                pairs.append((dev_id(x, y, core), dev_id(x + dx, y + dy, core)))
    return pairs


CORE_PAIRS = [(d, d ^ 1) for d in range(2 * X * Y)]


def move(value, first, shift):
    return lax.ppermute(value, "dev", ring_pairs(first, shift))


def move_group(value, shift):
    return lax.ppermute(value, "grp", [(g, (g + shift) % N_GRP) for g in range(N_GRP)])


def swap(value):
    return lax.ppermute(value, "dev", CORE_PAIRS)


def piece_blocks(z):
    base = []
    for d in range(N_DEV):
        x, y, core = d // (2 * Y), (d // 2) % Y, d % 2
        a, b = (x, y) if core == 0 else (y, x)
        base.append(((core * 4 + a) * 4 + b) * N_GRP)
    return jnp.asarray(base, jnp.int32) + z


def spread_kernel(width, block_ref, slot_ref, *refs):
    ins, out_ref = refs[:-1], refs[-1]
    for i in range(SPREAD):
        held = block_ref[pl.program_id(0) * SPREAD + i] < FILLED
        for s in range(width):
            rows = ins[i * width + s][...]
            out_ref[i, :, s * PB : (s + 1) * PB] = jnp.where(held, rows, jnp.zeros_like(rows))


def spread(factors, blocks, panel_in):
    width = panel_in.shape[0]

    def in_map(i, s, step, block_ref, panel_ref):
        return (jnp.minimum(block_ref[step * SPREAD + i], FILLED - 1), panel_ref[s])

    cols = width * PB
    return pl.pallas_call(
        functools.partial(spread_kernel, width),
        grid_spec=pltpu.PrefetchScalarGridSpec(
            num_scalar_prefetch=2,
            grid=(N_DEV // SPREAD,),
            in_specs=[
                pl.BlockSpec((PIECE, PB), functools.partial(in_map, i, s)) for i in range(SPREAD) for s in range(width)
            ],
            out_specs=pl.BlockSpec((SPREAD, PIECE, cols), lambda step, block_ref, panel_ref: (step, 0, 0)),
        ),
        out_shape=jax.ShapeDtypeStruct((N_DEV, PIECE, cols), jnp.bfloat16),
        compiler_params=pltpu.CompilerParams(vmem_limit_bytes=16 << 20),
        cost_estimate=pl.CostEstimate(flops=0, bytes_accessed=4 * N_DEV * PIECE * cols, transcendentals=0),
        name="spread_rows",
    )(blocks, panel_in, *([factors] * (SPREAD * width)))


def choose_kernel(source_ref, slot_ref, *refs):
    ins, outs = refs[:-N_GRP], refs[-N_GRP:]
    for i, in_ref in enumerate(ins):
        for h in range(CHUNKS):
            first = h * C + (i % PANELS) * W
            outs[i // PANELS][:, first : first + W] = in_ref[0, :, h * W : (h + 1) * W]


def choose(scattered, source, slot):
    count = N_GRP * PANELS

    def in_map(i, s, source_ref, slot_ref):
        return (source_ref[i], 0, slot_ref[i])

    return pl.pallas_call(
        choose_kernel,
        grid_spec=pltpu.PrefetchScalarGridSpec(
            num_scalar_prefetch=2,
            grid=(1,),
            in_specs=[pl.BlockSpec((1, PIECE, PB), functools.partial(in_map, i)) for i in range(count)],
            out_specs=[pl.BlockSpec((PIECE, CHUNKS * C), lambda s, source_ref, slot_ref: (0, 0))] * N_GRP,
        ),
        out_shape=[jax.ShapeDtypeStruct((PIECE, CHUNKS * C), jnp.bfloat16)] * N_GRP,
        compiler_params=pltpu.CompilerParams(vmem_limit_bytes=12 << 20),
        cost_estimate=pl.CostEstimate(flops=0, bytes_accessed=4 * count * PIECE * PB, transcendentals=0),
        name="choose_panels",
    )(source, slot, *([scattered] * count))


def join_kernel(z_ref, *refs):
    ins, outs = refs[:-CHUNKS], refs[-CHUNKS:]
    for shift, in_ref in enumerate(ins):
        at = lax.rem(z_ref[0] + N_GRP - shift, N_GRP)
        for h in range(CHUNKS):
            outs[h][at] = in_ref[:, h * C : (h + 1) * C]


def join(pieces, z):
    chunks = pl.pallas_call(
        join_kernel,
        grid_spec=pltpu.PrefetchScalarGridSpec(
            num_scalar_prefetch=1,
            grid=(1,),
            in_specs=[pl.BlockSpec((PIECE, CHUNKS * C), lambda s, z_ref: (0, 0))] * N_GRP,
            out_specs=[pl.BlockSpec((N_GRP, PIECE, C), lambda s, z_ref: (0, 0, 0))] * CHUNKS,
        ),
        out_shape=[jax.ShapeDtypeStruct((N_GRP, PIECE, C), jnp.bfloat16)] * CHUNKS,
        compiler_params=pltpu.CompilerParams(vmem_limit_bytes=12 << 20),
        cost_estimate=pl.CostEstimate(flops=0, bytes_accessed=4 * SIXT * CHUNKS * C, transcendentals=0),
        name="join_groups",
    )(z.reshape(1), *pieces)
    return [chunk.reshape(SIXT, C) for chunk in chunks]


def gather_window(panel_blocks, z):
    shape = (N_GRP, PANELS)
    mine = jnp.arange(N_GRP)[:, None]
    window = jnp.where(mine == z, panel_blocks[None, :], jnp.zeros(shape, jnp.int32))
    for shift in range(1, N_GRP):
        other = move_group(panel_blocks, shift)
        window = jnp.where(mine == (z - shift) % N_GRP, other[None, :], window)
    return window.reshape(-1)


def scatter_window(factors, window, me, z):
    panels = jnp.arange(N_DEV * PANELS)
    named = jnp.any(panels[:, None] == window[None, :], axis=1).reshape(N_DEV, PANELS).astype(jnp.int32)
    earlier = jnp.arange(PANELS)[None, :] < jnp.arange(PANELS)[:, None]
    slot = jnp.sum(jnp.where(earlier[None], named[:, None, :], 0), axis=2)
    most = jnp.max(jnp.sum(named, axis=1))
    source = window // PANELS
    hit = window[:, None] == panels[None, :]
    slot_of = jnp.sum(jnp.where(hit, slot.reshape(1, -1), 0), axis=1).astype(jnp.int32)
    own = (jnp.arange(N_DEV) == me)[:, None]
    my_named = jnp.sum(jnp.where(own, named, 0), axis=0)
    my_slot = jnp.sum(jnp.where(own, slot, 0), axis=0)
    fill = (my_named[None, :] == 1) & (my_slot[None, :] == jnp.arange(PANELS)[:, None])
    panel_in = jnp.sum(jnp.where(fill, jnp.arange(PANELS)[None, :], 0), axis=1).astype(jnp.int32)
    blocks = piece_blocks(z)
    turned = jnp.arange(N_GRP * PANELS)[None, :] == ((jnp.arange(N_GRP * PANELS) + z * PANELS) % (N_GRP * PANELS))[:, None]
    source = jnp.sum(jnp.where(turned, source[None, :], 0), axis=1).astype(jnp.int32)
    slot_of = jnp.sum(jnp.where(turned, slot_of[None, :], 0), axis=1).astype(jnp.int32)

    def with_slots(width):
        def run(blocks, panel_in, source, slot_of):
            leaving = spread(factors, blocks, panel_in[:width])
            scattered = lax.all_to_all(leaving, "dev", split_axis=0, concat_axis=0, tiled=True)
            return choose(scattered, source, slot_of)

        return run

    branches = [with_slots(width) for width in range(1, PANELS + 1)]
    return lax.switch(most - 1, branches, blocks, panel_in, source, slot_of)


def multiply_kernel(items, before, sides, slots, through, *refs):
    place_ref, refs = refs[0], refs[1:]
    if slots:
        (tile_ref, scale_ref), refs = refs[:2], refs[2:]
    count = len(items)
    values, refs = refs[:count], refs[count:]
    factor_refs, end_refs, refs = refs[:sides], refs[sides : 2 * sides], refs[2 * sides :]
    before_refs, refs = refs[:before], refs[before:]
    if slots:
        out_ref, total_refs, refs = refs[0], refs[1 : 1 + CHUNKS], refs[1 + CHUNKS :]
    else:
        total_refs, refs = refs[: CHUNKS * sides], refs[CHUNKS * sides + through :]
    held_ref, rows_ref, value_sems, row_sems = refs
    last = NAUX // QUART
    even = NAUX // 16 * 16 - last * QUART
    copies = [pltpu.make_async_copy(values[i], held_ref.at[i], value_sems.at[i]) for i in range(count)]

    def rows(j, side, size):
        start = pl.multiple_of(place_ref[j] * QUART, QUART)
        at = j * sides + side
        return pltpu.make_async_copy(
            factor_refs[side].at[pl.ds(start, size)], rows_ref.at[at, pl.ds(0, size)], row_sems.at[at]
        )

    def by_place(j, whole, end):
        pl.when(place_ref[j] != last)(whole)
        pl.when(place_ref[j] == last)(end)

    def fetch(j, side):
        def end():
            ends = end_refs[side][...]
            inside = lax.broadcasted_iota(jnp.int32, ends.shape, 0) < NAUX % 16
            rows_ref[j * sides + side, even : even + 16] = jnp.where(inside, ends, jnp.zeros_like(ends))
            rows(j, side, even).start()

        by_place(j, lambda: rows(j, side, QUART).start(), end)

    fetched = set()
    for i, (_, j) in enumerate(items):
        copies[i].start()
        if j not in fetched:
            fetched.add(j)
            for side in range(sides):
                fetch(j, side)

    def add(i, side, size):
        h, j = items[i]
        part = lax.dot_general(
            held_ref[i, :size],
            rows_ref[j * sides + side, :size],
            (((0,), (0,)), ((), ())),
            preferred_element_type=jnp.float32,
        )
        at = CHUNKS * side + h
        if any(chunk == h for chunk, _ in items[:i]):
            part += total_refs[at][...]
        else:
            for before_ref in before_refs[at :: CHUNKS * sides]:
                part += before_ref[...]
        total_refs[at][...] = part

    waited = set()
    for i, (_, j) in enumerate(items):
        copies[i].wait()
        for side in range(sides):
            if (j, side) not in waited:
                waited.add((j, side))
                by_place(
                    j,
                    lambda j=j, side=side: rows(j, side, QUART).wait(),
                    lambda j=j, side=side: rows(j, side, even).wait(),
                )
            by_place(
                j,
                lambda i=i, side=side: add(i, side, QUART),
                lambda i=i, side=side: add(i, side, even + 16),
            )

    if slots:

        def slot(s, carry):
            t = tile_ref[s]
            row = pl.multiple_of((t // 8) * W, W)
            col = pl.multiple_of((t % 8) * CB, CB)
            for h in range(CHUNKS):
                block = total_refs[h][pl.ds(row, W), pl.ds(col, CB)]
                out_ref[s, h * W : (h + 1) * W, :] = (block * scale_ref[s]).astype(jnp.bfloat16)
            return carry

        lax.fori_loop(0, slots, slot, 0, unroll=8)


def multiply(before, items, arrays, places, factors, table=None, through=0):
    count, cols, sides = len(items), factors[0].shape[1], len(factors)
    slots = 0 if table is None else table[0].shape[0]
    kept = len(places) * sides
    places = jnp.stack([jnp.asarray(p, jnp.int32) for p in places])
    vmem, anywhere = pl.BlockSpec(memory_space=pltpu.VMEM), pl.BlockSpec(memory_space=pl.ANY)
    ends = pl.BlockSpec((16, cols), lambda s: (NAUX // 16, 0))
    smem = pl.BlockSpec(memory_space=pltpu.SMEM)
    in_specs, operands = [smem], [places]
    if slots:
        in_specs += [smem] * 2
        operands += list(table)
    in_specs += [anywhere] * (count + sides) + [ends] * sides + [vmem] * len(before)
    operands += [*arrays, *factors, *factors, *before]
    aliases = {}
    if slots:
        out_specs, out_shape = vmem, jax.ShapeDtypeStruct((slots, PB, CB), jnp.bfloat16)
    else:
        sums = CHUNKS * sides
        out_specs = [vmem] * sums + [anywhere] * through
        out_shape = [jax.ShapeDtypeStruct((C, cols), jnp.float32)] * sums
        out_shape += [jax.ShapeDtypeStruct(array.shape, array.dtype) for array in arrays[:through]]
        aliases.update({1 + i: sums + i for i in range(through)})
    scratch = [pltpu.VMEM((C, cols), jnp.float32)] * CHUNKS if slots else []
    scratch += [
        pltpu.VMEM((count, QUART, C), jnp.bfloat16),
        pltpu.VMEM((kept, QUART, cols), jnp.bfloat16),
        pltpu.SemaphoreType.DMA((count,)),
        pltpu.SemaphoreType.DMA((kept,)),
    ]
    moved = 2 * count * QUART * (C + sides * cols)
    return pl.pallas_call(
        functools.partial(multiply_kernel, items, len(before), sides, slots, through),
        grid=(1,),
        in_specs=in_specs,
        out_specs=out_specs,
        out_shape=out_shape,
        scratch_shapes=scratch,
        input_output_aliases=aliases,
        compiler_params=pltpu.CompilerParams(vmem_limit_bytes=(26 if slots else 24) << 20),
        cost_estimate=pl.CostEstimate(flops=2 * count * sides * QUART * C * cols, bytes_accessed=moved, transcendentals=0),
        name="multiply_slots" if slots else "multiply",
    )(*operands)


def place_kernel(at_ref, *refs):
    ins, outs = refs[:-CHUNKS], refs[-CHUNKS:]
    for i, in_ref in enumerate(ins):
        start = pl.multiple_of(at_ref[i // CHUNKS] * SIXT, SIXT)
        outs[i % CHUNKS][pl.ds(start, SIXT), :] = in_ref[...]


def place(pieces, places):
    arrays = [array for piece in pieces for array in piece]
    whole = pl.BlockSpec((QUART, C), lambda s, at_ref: (0, 0))
    return pl.pallas_call(
        place_kernel,
        grid_spec=pltpu.PrefetchScalarGridSpec(
            num_scalar_prefetch=1,
            grid=(1,),
            in_specs=[pl.BlockSpec((SIXT, C), lambda s, at_ref: (0, 0))] * len(arrays),
            out_specs=[whole] * CHUNKS,
        ),
        out_shape=[jax.ShapeDtypeStruct((QUART, C), jnp.bfloat16)] * CHUNKS,
        compiler_params=pltpu.CompilerParams(vmem_limit_bytes=16 << 20),
        cost_estimate=pl.CostEstimate(flops=0, bytes_accessed=4 * QUART * C * CHUNKS, transcendentals=0),
        name="place_pieces",
    )(jnp.stack(places).astype(jnp.int32), *arrays)


def slot_table(owners, slots, kept):
    count = owners.shape[0]
    same_owner = owners[:, None] == owners[None, :]
    earlier = jnp.arange(count)[None, :] < jnp.arange(count)[:, None]
    ranks = jnp.sum((same_owner & earlier).astype(jnp.int32), axis=-1)
    hit = (owners * 2 + ranks)[None, :] == jnp.arange(slots)[:, None]
    tile_of = jnp.sum(jnp.where(hit, jnp.arange(count)[None, :], 0), axis=1).astype(jnp.int32)
    scale_of = jnp.sum(jnp.where(hit, kept[None, :], 0), axis=1).astype(jnp.float32)
    return tile_of, scale_of


def body(fitted_factors, panel_blocks, kept_tiles, tile_owner):
    me, z = lax.axis_index("dev"), lax.axis_index("grp")
    core = me % 2
    mx, my = me // (2 * Y), (me // 2) % Y
    here_a, here_b = jnp.where(core == 0, mx, my), jnp.where(core == 0, my, mx)
    window = gather_window(panel_blocks, z)

    slots = 2 * N_DEV
    table = slot_table(tile_owner[0, 0, :, 0], slots, kept_tiles.reshape(-1))
    sibling_factors = swap(fitted_factors)
    chosen = scatter_window(fitted_factors, window, me, z)
    pieces = [chosen[0]] + [move_group(chosen[shift], shift) for shift in range(1, N_GRP)]
    sixteenth = join(pieces, z)
    first, second = sixteenth
    behind_first, ahead_second = move(first, False, 1), move(second, False, -1)
    ahead_first, behind_second = move(first, False, -1), move(second, False, 1)
    across_first, across_second = move(behind_first, False, 1), move(ahead_second, False, -1)
    quarts = place(
        [
            (first, second),
            (behind_first, behind_second),
            (ahead_first, ahead_second),
            (across_first, across_second),
        ],
        [here_b, (here_b + 3) % 4, (here_b + 1) % 4, (here_b + 2) % 4],
    )

    def slice_of(core_of, a_of):
        return core_of * 4 + a_of % 4

    def add(before, arrays, places, factors, table=None, through=0):
        items = [(i % CHUNKS, i if len(places) > 1 else 0) for i in range(len(arrays))]
        return multiply(before, items, arrays, places, factors, table, through)

    first, second = quarts
    here, behind, ahead, far = [slice_of(core, here_a + step) for step in (0, 3, 1, 2)]
    other_far = slice_of(1 - core, here_b + 2)
    factors = [fitted_factors, sibling_factors]
    behind_first, ahead_second = move(first, True, 1), move(second, True, -1)
    ahead_first, behind_second = move(first, True, -1), move(second, True, 1)
    sums = add([], [first, second], [here], factors)
    *sums, behind_first, ahead_second = add(sums, [behind_first, ahead_second], [behind, ahead], factors, through=2)
    far_first, far_second = move(behind_first, True, 1), move(ahead_second, True, -1)
    sums = add(sums, [ahead_first, behind_second], [ahead, behind], factors)
    own, other = sums[:CHUNKS], sums[CHUNKS:]
    own = add(own, [far_first, far_second], [far], factors[:1])
    outgoing = add(
        [*own, *[swap(value) for value in other]],
        [swap(far_first), swap(far_second)],
        [other_far],
        factors[:1],
        table,
    )
    exported = lax.all_to_all(outgoing, "dev", split_axis=0, concat_axis=0, tiled=True)
    return exported.reshape(1, 1, slots, PB, CB)


def solution(mesh):
    placed = (P(None, "dev"), P("grp"), P("grp", "dev"), P("grp", "dev", None, None))
    return jax.shard_map(
        body,
        mesh=mesh,
        in_specs=placed,
        out_specs=P("grp", "dev", None, None, None),
        check_vma=False,
    )
```

```python
import functools

import jax
import jax.numpy as jnp
from jax import lax
from jax.experimental import pallas as pl
from jax.experimental.pallas import tpu as pltpu
from jax.sharding import PartitionSpec as P

PB = 256
CB = 128
W = 128
CHUNKS = PB // W
PANELS = 4
C = PANELS * W
NAUX = 9000
HALF = 4608
QUART = HALF // 4
SIXT = QUART // 4
X, Y = 4, 4
N_DEV = 2 * X * Y
N_GRP = 4
PIECE = SIXT // N_GRP
SPREAD = 8
FILLED = NAUX // PIECE


def dev_id(x, y, core):
    return ((x % X) * Y + (y % Y)) * 2 + core


def ring_pairs(first, shift):
    pairs = []
    for x in range(X):
        for y in range(Y):
            for core in range(2):
                along_x = first == (core == 0)
                dx, dy = (shift, 0) if along_x else (0, shift)
                pairs.append((dev_id(x, y, core), dev_id(x + dx, y + dy, core)))
    return pairs


CORE_PAIRS = [(d, d ^ 1) for d in range(2 * X * Y)]


def move(value, first, shift):
    return lax.ppermute(value, "dev", ring_pairs(first, shift))


def move_group(value, shift):
    return lax.ppermute(value, "grp", [(g, (g + shift) % N_GRP) for g in range(N_GRP)])


def swap(value):
    return lax.ppermute(value, "dev", CORE_PAIRS)


def piece_blocks(z):
    base = []
    for d in range(N_DEV):
        x, y, core = d // (2 * Y), (d // 2) % Y, d % 2
        a, b = (x, y) if core == 0 else (y, x)
        base.append(((core * 4 + a) * 4 + b) * N_GRP)
    return jnp.asarray(base, jnp.int32) + z


def spread_kernel(width, block_ref, slot_ref, *refs):
    ins, out_ref = refs[:-1], refs[-1]
    for i in range(SPREAD):
        held = block_ref[pl.program_id(0) * SPREAD + i] < FILLED
        for s in range(width):
            rows = ins[i * width + s][...]
            out_ref[i, :, s * PB : (s + 1) * PB] = jnp.where(held, rows, jnp.zeros_like(rows))


def spread(factors, blocks, panel_in):
    width = panel_in.shape[0]

    def in_map(i, s, step, block_ref, panel_ref):
        return (jnp.minimum(block_ref[step * SPREAD + i], FILLED - 1), panel_ref[s])

    cols = width * PB
    return pl.pallas_call(
        functools.partial(spread_kernel, width),
        grid_spec=pltpu.PrefetchScalarGridSpec(
            num_scalar_prefetch=2,
            grid=(N_DEV // SPREAD,),
            in_specs=[
                pl.BlockSpec((PIECE, PB), functools.partial(in_map, i, s)) for i in range(SPREAD) for s in range(width)
            ],
            out_specs=pl.BlockSpec((SPREAD, PIECE, cols), lambda step, block_ref, panel_ref: (step, 0, 0)),
        ),
        out_shape=jax.ShapeDtypeStruct((N_DEV, PIECE, cols), jnp.bfloat16),
        compiler_params=pltpu.CompilerParams(vmem_limit_bytes=16 << 20),
        cost_estimate=pl.CostEstimate(flops=0, bytes_accessed=4 * N_DEV * PIECE * cols, transcendentals=0),
        name="spread_rows",
    )(blocks, panel_in, *([factors] * (SPREAD * width)))


def choose_kernel(source_ref, slot_ref, *refs):
    ins, outs = refs[:-N_GRP], refs[-N_GRP:]
    for i, in_ref in enumerate(ins):
        for h in range(CHUNKS):
            first = h * C + (i % PANELS) * W
            outs[i // PANELS][:, first : first + W] = in_ref[0, :, h * W : (h + 1) * W]


def choose(scattered, source, slot):
    count = N_GRP * PANELS

    def in_map(i, s, source_ref, slot_ref):
        return (source_ref[i], 0, slot_ref[i])

    return pl.pallas_call(
        choose_kernel,
        grid_spec=pltpu.PrefetchScalarGridSpec(
            num_scalar_prefetch=2,
            grid=(1,),
            in_specs=[pl.BlockSpec((1, PIECE, PB), functools.partial(in_map, i)) for i in range(count)],
            out_specs=[pl.BlockSpec((PIECE, CHUNKS * C), lambda s, source_ref, slot_ref: (0, 0))] * N_GRP,
        ),
        out_shape=[jax.ShapeDtypeStruct((PIECE, CHUNKS * C), jnp.bfloat16)] * N_GRP,
        compiler_params=pltpu.CompilerParams(vmem_limit_bytes=12 << 20),
        cost_estimate=pl.CostEstimate(flops=0, bytes_accessed=4 * count * PIECE * PB, transcendentals=0),
        name="choose_panels",
    )(source, slot, *([scattered] * count))


def join_kernel(z_ref, *refs):
    ins, outs = refs[:-CHUNKS], refs[-CHUNKS:]
    for shift, in_ref in enumerate(ins):
        at = lax.rem(z_ref[0] + N_GRP - shift, N_GRP)
        for h in range(CHUNKS):
            outs[h][at] = in_ref[:, h * C : (h + 1) * C]


def join(pieces, z):
    chunks = pl.pallas_call(
        join_kernel,
        grid_spec=pltpu.PrefetchScalarGridSpec(
            num_scalar_prefetch=1,
            grid=(1,),
            in_specs=[pl.BlockSpec((PIECE, CHUNKS * C), lambda s, z_ref: (0, 0))] * N_GRP,
            out_specs=[pl.BlockSpec((N_GRP, PIECE, C), lambda s, z_ref: (0, 0, 0))] * CHUNKS,
        ),
        out_shape=[jax.ShapeDtypeStruct((N_GRP, PIECE, C), jnp.bfloat16)] * CHUNKS,
        compiler_params=pltpu.CompilerParams(vmem_limit_bytes=12 << 20),
        cost_estimate=pl.CostEstimate(flops=0, bytes_accessed=4 * SIXT * CHUNKS * C, transcendentals=0),
        name="join_groups",
    )(z.reshape(1), *pieces)
    return [chunk.reshape(SIXT, C) for chunk in chunks]


def gather_window(panel_blocks, z):
    shape = (N_GRP, PANELS)
    mine = jnp.arange(N_GRP)[:, None]
    window = jnp.where(mine == z, panel_blocks[None, :], jnp.zeros(shape, jnp.int32))
    for shift in range(1, N_GRP):
        other = move_group(panel_blocks, shift)
        window = jnp.where(mine == (z - shift) % N_GRP, other[None, :], window)
    return window.reshape(-1)


def scatter_window(factors, window, me, z):
    panels = jnp.arange(N_DEV * PANELS)
    named = jnp.any(panels[:, None] == window[None, :], axis=1).reshape(N_DEV, PANELS).astype(jnp.int32)
    earlier = jnp.arange(PANELS)[None, :] < jnp.arange(PANELS)[:, None]
    slot = jnp.sum(jnp.where(earlier[None], named[:, None, :], 0), axis=2)
    most = jnp.max(jnp.sum(named, axis=1))
    source = window // PANELS
    hit = window[:, None] == panels[None, :]
    slot_of = jnp.sum(jnp.where(hit, slot.reshape(1, -1), 0), axis=1).astype(jnp.int32)
    own = (jnp.arange(N_DEV) == me)[:, None]
    my_named = jnp.sum(jnp.where(own, named, 0), axis=0)
    my_slot = jnp.sum(jnp.where(own, slot, 0), axis=0)
    fill = (my_named[None, :] == 1) & (my_slot[None, :] == jnp.arange(PANELS)[:, None])
    panel_in = jnp.sum(jnp.where(fill, jnp.arange(PANELS)[None, :], 0), axis=1).astype(jnp.int32)
    blocks = piece_blocks(z)
    turned = jnp.arange(N_GRP * PANELS)[None, :] == ((jnp.arange(N_GRP * PANELS) + z * PANELS) % (N_GRP * PANELS))[:, None]
    source = jnp.sum(jnp.where(turned, source[None, :], 0), axis=1).astype(jnp.int32)
    slot_of = jnp.sum(jnp.where(turned, slot_of[None, :], 0), axis=1).astype(jnp.int32)

    def with_slots(width):
        def run(blocks, panel_in, source, slot_of):
            leaving = spread(factors, blocks, panel_in[:width])
            scattered = lax.all_to_all(leaving, "dev", split_axis=0, concat_axis=0, tiled=True)
            return choose(scattered, source, slot_of)

        return run

    branches = [with_slots(width) for width in range(1, PANELS + 1)]
    return lax.switch(most - 1, branches, blocks, panel_in, source, slot_of)


def multiply_kernel(items, before, sides, slots, through, *refs):
    place_ref, refs = refs[0], refs[1:]
    if slots:
        (tile_ref, scale_ref), refs = refs[:2], refs[2:]
    count = len(items)
    values, refs = refs[:count], refs[count:]
    factor_refs, end_refs, refs = refs[:sides], refs[sides : 2 * sides], refs[2 * sides :]
    before_refs, refs = refs[:before], refs[before:]
    if slots:
        out_ref, refs = refs[0], refs[1:]
    else:
        sum_refs, refs = refs[: CHUNKS * sides], refs[CHUNKS * sides :]
    again_refs, refs = refs[:through], refs[through:]
    total_refs, refs = refs[: max(before, CHUNKS * sides)], refs[max(before, CHUNKS * sides) :]
    held_ref, rows_ref, value_sems, row_sems, again_sems, before_sems, sum_sems = refs
    loads = [pltpu.make_async_copy(before_refs[i], total_refs[i], before_sems.at[i]) for i in range(before)]
    stores = []
    last = NAUX // QUART
    even = NAUX // 16 * 16 - last * QUART
    copies = [pltpu.make_async_copy(values[i], held_ref.at[i], value_sems.at[i]) for i in range(count)]

    again = [
        pltpu.make_async_copy(held_ref.at[i], again_refs[i], again_sems.at[i]) for i in range(through)
    ]

    def rows(j, side, size):
        start = pl.multiple_of(place_ref[j] * QUART, QUART)
        at = j * sides + side
        return pltpu.make_async_copy(
            factor_refs[side].at[pl.ds(start, size)], rows_ref.at[at, pl.ds(0, size)], row_sems.at[at]
        )

    def by_place(j, whole, end):
        pl.when(place_ref[j] != last)(whole)
        pl.when(place_ref[j] == last)(end)

    def fetch(j, side):
        def end():
            ends = end_refs[side][...]
            inside = lax.broadcasted_iota(jnp.int32, ends.shape, 0) < NAUX % 16
            rows_ref[j * sides + side, even : even + 16] = jnp.where(inside, ends, jnp.zeros_like(ends))
            rows(j, side, even).start()

        by_place(j, lambda: rows(j, side, QUART).start(), end)

    fetched = set()
    for i, (_, j) in enumerate(items):
        copies[i].start()
        if j not in fetched:
            fetched.add(j)
            for side in range(sides):
                fetch(j, side)
        if i == 0:
            for load in loads:
                load.start()

    def add(i, side, size):
        h, j = items[i]
        part = lax.dot_general(
            held_ref[i, :size],
            rows_ref[j * sides + side, :size],
            (((0,), (0,)), ((), ())),
            preferred_element_type=jnp.float32,
        )
        at = CHUNKS * side + h
        if any(chunk == h for chunk, _ in items[:i]):
            part += total_refs[at][...]
        else:
            for before_ref in total_refs[at : before : CHUNKS * sides]:
                part += before_ref[...]
        total_refs[at][...] = part

    waited = set()
    for i, (_, j) in enumerate(items):
        copies[i].wait()
        if i < through:
            again[i].start()
        for side in range(sides):
            if (j, side) not in waited:
                waited.add((j, side))
                by_place(
                    j,
                    lambda j=j, side=side: rows(j, side, QUART).wait(),
                    lambda j=j, side=side: rows(j, side, even).wait(),
                )
            at = CHUNKS * side + items[i][0]
            if all(chunk != items[i][0] for chunk, _ in items[:i]):
                for load in loads[at :: CHUNKS * sides]:
                    load.wait()
            by_place(
                j,
                lambda i=i, side=side: add(i, side, QUART),
                lambda i=i, side=side: add(i, side, even + 16),
            )
            if not slots and all(chunk != items[i][0] for chunk, _ in items[i + 1 :]):
                stores.append(pltpu.make_async_copy(total_refs[at], sum_refs[at], sum_sems.at[at]))
                stores[-1].start()

    for copy in [*again, *stores]:
        copy.wait()

    if slots:

        def slot(s, carry):
            t = tile_ref[s]
            row = pl.multiple_of((t // 8) * W, W)
            col = pl.multiple_of((t % 8) * CB, CB)
            for h in range(CHUNKS):
                block = total_refs[h][pl.ds(row, W), pl.ds(col, CB)]
                out_ref[s, h * W : (h + 1) * W, :] = (block * scale_ref[s]).astype(jnp.bfloat16)
            return carry

        lax.fori_loop(0, slots, slot, 0, unroll=8)


def multiply(before, items, arrays, places, factors, table=None, through=0):
    count, cols, sides = len(items), factors[0].shape[1], len(factors)
    slots = 0 if table is None else table[0].shape[0]
    kept = len(places) * sides
    places = jnp.stack([jnp.asarray(p, jnp.int32) for p in places])
    vmem, anywhere = pl.BlockSpec(memory_space=pltpu.VMEM), pl.BlockSpec(memory_space=pl.ANY)
    ends = pl.BlockSpec((16, cols), lambda s: (NAUX // 16, 0))
    smem = pl.BlockSpec(memory_space=pltpu.SMEM)
    in_specs, operands = [smem], [places]
    if slots:
        in_specs += [smem] * 2
        operands += list(table)
    in_specs += [anywhere] * (count + sides) + [ends] * sides + [anywhere] * len(before)
    operands += [*arrays, *factors, *factors, *before]
    if slots:
        out_specs, out_shape = vmem, jax.ShapeDtypeStruct((slots, PB, CB), jnp.bfloat16)
    else:
        sums = CHUNKS * sides
        out_specs = [anywhere] * (sums + through)
        out_shape = [jax.ShapeDtypeStruct((C, cols), jnp.float32)] * sums
        out_shape += [jax.ShapeDtypeStruct(array.shape, array.dtype) for array in arrays[:through]]
    scratch = [pltpu.VMEM((C, cols), jnp.float32)] * max(len(before), CHUNKS * sides)
    scratch += [
        pltpu.VMEM((count, QUART, C), jnp.bfloat16),
        pltpu.VMEM((kept, QUART, cols), jnp.bfloat16),
        pltpu.SemaphoreType.DMA((count,)),
        pltpu.SemaphoreType.DMA((kept,)),
        pltpu.SemaphoreType.DMA((max(through, 1),)),
        pltpu.SemaphoreType.DMA((max(len(before), 1),)),
        pltpu.SemaphoreType.DMA((CHUNKS * sides,)),
    ]
    moved = 2 * count * QUART * (C + sides * cols)
    return pl.pallas_call(
        functools.partial(multiply_kernel, items, len(before), sides, slots, through),
        grid=(1,),
        in_specs=in_specs,
        out_specs=out_specs,
        out_shape=out_shape,
        scratch_shapes=scratch,
        compiler_params=pltpu.CompilerParams(vmem_limit_bytes=34 << 20),
        cost_estimate=pl.CostEstimate(flops=2 * count * sides * QUART * C * cols, bytes_accessed=moved, transcendentals=0),
        name="multiply_slots" if slots else "multiply",
    )(*operands)


def place_kernel(at_ref, *refs):
    ins, outs = refs[:-CHUNKS], refs[-CHUNKS:]
    for i, in_ref in enumerate(ins):
        start = pl.multiple_of(at_ref[i // CHUNKS] * SIXT, SIXT)
        outs[i % CHUNKS][pl.ds(start, SIXT), :] = in_ref[...]


def place(pieces, places):
    arrays = [array for piece in pieces for array in piece]
    whole = pl.BlockSpec((QUART, C), lambda s, at_ref: (0, 0))
    return pl.pallas_call(
        place_kernel,
        grid_spec=pltpu.PrefetchScalarGridSpec(
            num_scalar_prefetch=1,
            grid=(1,),
            in_specs=[pl.BlockSpec((SIXT, C), lambda s, at_ref: (0, 0))] * len(arrays),
            out_specs=[whole] * CHUNKS,
        ),
        out_shape=[jax.ShapeDtypeStruct((QUART, C), jnp.bfloat16)] * CHUNKS,
        compiler_params=pltpu.CompilerParams(vmem_limit_bytes=16 << 20),
        cost_estimate=pl.CostEstimate(flops=0, bytes_accessed=4 * QUART * C * CHUNKS, transcendentals=0),
        name="place_pieces",
    )(jnp.stack(places).astype(jnp.int32), *arrays)


def slot_table(owners, slots, kept):
    count = owners.shape[0]
    same_owner = owners[:, None] == owners[None, :]
    earlier = jnp.arange(count)[None, :] < jnp.arange(count)[:, None]
    ranks = jnp.sum((same_owner & earlier).astype(jnp.int32), axis=-1)
    hit = (owners * 2 + ranks)[None, :] == jnp.arange(slots)[:, None]
    tile_of = jnp.sum(jnp.where(hit, jnp.arange(count)[None, :], 0), axis=1).astype(jnp.int32)
    scale_of = jnp.sum(jnp.where(hit, kept[None, :], 0), axis=1).astype(jnp.float32)
    return tile_of, scale_of


def body(fitted_factors, panel_blocks, kept_tiles, tile_owner):
    me, z = lax.axis_index("dev"), lax.axis_index("grp")
    core = me % 2
    mx, my = me // (2 * Y), (me // 2) % Y
    here_a, here_b = jnp.where(core == 0, mx, my), jnp.where(core == 0, my, mx)
    window = gather_window(panel_blocks, z)

    slots = 2 * N_DEV
    table = slot_table(tile_owner[0, 0, :, 0], slots, kept_tiles.reshape(-1))
    sibling_factors = swap(fitted_factors)
    chosen = scatter_window(fitted_factors, window, me, z)
    pieces = [chosen[0]] + [move_group(chosen[shift], shift) for shift in range(1, N_GRP)]
    sixteenth = join(pieces, z)
    first, second = sixteenth
    behind_first, ahead_second = move(first, False, 1), move(second, False, -1)
    ahead_first, behind_second = move(first, False, -1), move(second, False, 1)
    across_first, across_second = move(behind_first, False, 1), move(ahead_second, False, -1)
    quarts = place(
        [
            (first, second),
            (behind_first, behind_second),
            (ahead_first, ahead_second),
            (across_first, across_second),
        ],
        [here_b, (here_b + 3) % 4, (here_b + 1) % 4, (here_b + 2) % 4],
    )

    def slice_of(core_of, a_of):
        return core_of * 4 + a_of % 4

    def add(before, arrays, places, factors, table=None, through=0):
        items = [(i % CHUNKS, i if len(places) > 1 else 0) for i in range(len(arrays))]
        return multiply(before, items, arrays, places, factors, table, through)

    first, second = quarts
    here, behind, ahead, far = [slice_of(core, here_a + step) for step in (0, 3, 1, 2)]
    other_far = slice_of(1 - core, here_b + 2)
    factors = [fitted_factors, sibling_factors]
    behind_first, ahead_second = move(first, True, 1), move(second, True, -1)
    ahead_first, behind_second = move(first, True, -1), move(second, True, 1)
    sums = add([], [first, second], [here], factors)
    *sums, behind_first, ahead_second = add(sums, [behind_first, ahead_second], [behind, ahead], factors, through=2)
    far_first, far_second = move(behind_first, True, 1), move(ahead_second, True, -1)
    sums = add(sums, [ahead_first, behind_second], [ahead, behind], factors)
    own, other = sums[:CHUNKS], sums[CHUNKS:]
    own = add(own, [far_first, far_second], [far], factors[:1])
    outgoing = add(
        [*own, *[swap(value) for value in other]],
        [swap(far_first), swap(far_second)],
        [other_far],
        factors[:1],
        table,
    )
    exported = lax.all_to_all(outgoing, "dev", split_axis=0, concat_axis=0, tiled=True)
    return exported.reshape(1, 1, slots, PB, CB)


def solution(mesh):
    placed = (P(None, "dev"), P("grp"), P("grp", "dev"), P("grp", "dev", None, None))
    return jax.shard_map(
        body,
        mesh=mesh,
        in_specs=placed,
        out_specs=P("grp", "dev", None, None, None),
        check_vma=False,
    )
```
